32 devices in a mesh: chan: 8 (over z, x), win: 4 (over y, core).
Axes of the slice: x: 2, y: 2, z: 4, core: 2. Of those that a mesh axis runs over, the one named last changes fastest.
Arguments:
- spectra: bfloat16 [2, 8, 512, 1024], P(None, 'win', 'chan'), may hold values from -200 to 200
- pair_blocks: int32 [32, 2], P(('chan', 'win')), may hold values from 0 to 7, as said below
Outputs:
- stacks: float32 [32, 64, 64, 256], P(('chan', 'win'))
The draws below stay inside these ranges and needn't reach their ends.
Inputs may be any that keep to these rules, and one draw needn't show every extreme that they name: `pair_blocks`: row p belongs to channel block c = p // 4. The 4 rows of c hold, in a drawn order and each in a drawn orientation, the pairs of blocks c - d // 2 and c - d // 2 + d for d = 0 to 3, block numbers taken modulo 8; so every pair of blocks at cyclic distance below 4 appears exactly once in all.
All inputs are finite; a program needn't handle non-finite values.
Results may differ from the reference program's by a relative error of at most 0.0032.
Values may be sent and summed in bfloat16 or wider, within the bound.
A program may use at most 256 MiB of HBM per device.

```python
import math
import jax
import jax.numpy as jnp
from jax import lax

CH = 64
F = 1024
NLAG = 256
BLOCKS = 8
CHANNELS = 512
WINDOWS = 8
OWNER_ROWS = 4
NPB = 32
HALF_BAND = 64


def draw_spectra(key, part):
    key_base, key_level, key_rate, key_phase = jax.random.split(jax.random.fold_in(key, 7), 4)
    full_shape = (2, WINDOWS, CHANNELS, F)
    base = jnp.clip(jax.random.normal(key_base, full_shape, jnp.float32), -6.0, 6.0)
    level = 10.0 ** jax.random.uniform(key_level, (1, 1, CHANNELS, 1), jnp.float32, 0.0, 1.0)
    depth = 1.2
    rates = jax.random.uniform(key_rate, (1, 1, CHANNELS, 1), jnp.float32, 0.5, 3.0)
    phases = jax.random.uniform(key_phase, (1, 1, CHANNELS, 1), jnp.float32, 0.0, 2.0 * math.pi)
    bin_pos = jnp.arange(F, dtype=jnp.float32) / F
    tilt = jnp.exp(depth * jnp.sin(2.0 * math.pi * rates * bin_pos + phases))
    return (base * level * tilt).astype(jnp.bfloat16)


def draw_pair_blocks(key, part):
    key_order, key_flip = jax.random.split(jax.random.fold_in(key, 11))
    slots = jnp.arange(OWNER_ROWS, dtype=jnp.int32)
    scores = jax.random.randint(key_order, (BLOCKS, OWNER_ROWS), 0, 1048576) * OWNER_ROWS + slots[None, :]
    spacing = jnp.argsort(scores, axis=1, stable=True).astype(jnp.int32)
    owner = jnp.arange(BLOCKS, dtype=jnp.int32)[:, None]
    leading = owner - spacing // 2
    trailing = leading + spacing
    leading = jnp.mod(leading, BLOCKS).reshape(-1)
    trailing = jnp.mod(trailing, BLOCKS).reshape(-1)
    flip = jax.random.randint(key_flip, (NPB,), 0, 2)
    first = jnp.where(flip == 1, trailing, leading)
    second = jnp.where(flip == 1, leading, trailing)
    return jnp.stack([first, second], axis=1).astype(jnp.int32)


def setup_inputs(seed: int = 0) -> dict:
    arg_keys = jax.random.split(jax.random.key(seed), 3)
    spectra = draw_spectra(jax.random.fold_in(arg_keys[2], 71), 0)
    pair_blocks = draw_pair_blocks(jax.random.fold_in(arg_keys[2], 71), 0)
    return {"spectra": spectra, "pair_blocks": pair_blocks}


eps = 1e-05
first_bin = 60.0
samples = 15000.0

def smoothing(length_bins, half_width):
    indices = jnp.arange(length_bins, dtype=jnp.int32)
    return (jnp.abs(indices[:, None] - indices[None, :]) <= half_width).astype(jnp.float32)

def whiten(spectra):
    real_part = spectra[0].astype(jnp.float32)
    imag_part = spectra[1].astype(jnp.float32)
    powers = real_part * real_part + imag_part * imag_part
    smoother = smoothing(F, HALF_BAND)
    counts = lax.optimization_barrier(jnp.sum(smoother, axis=0))
    rows_flat = powers.reshape(-1, F)
    smooth = jnp.dot(rows_flat, smoother, precision=lax.Precision.HIGHEST) / counts
    factor = lax.rsqrt(smooth + eps).reshape(powers.shape)
    return jnp.stack([real_part * factor, imag_part * factor]).astype(jnp.bfloat16)

def make_table():
    bin_freq = first_bin + jnp.arange(F, dtype=jnp.float32)
    lag_steps = jnp.arange(NLAG, dtype=jnp.float32) - NLAG // 2
    angles = 2.0 * math.pi / samples * bin_freq[:, None] * lag_steps[None, :]
    return jnp.concatenate([jnp.cos(angles), -jnp.sin(angles)], axis=0).astype(jnp.bfloat16)

def cross_spectrum(leading, trailing):
    left_side = leading.astype(jnp.float32)
    right_side = trailing.astype(jnp.float32)
    real_sum = jnp.einsum('wif,wjf->ijf', left_side[0], right_side[0]) + jnp.einsum('wif,wjf->ijf', left_side[1], right_side[1])
    imag_sum = jnp.einsum('wif,wjf->ijf', left_side[1], right_side[0]) - jnp.einsum('wif,wjf->ijf', left_side[0], right_side[1])
    return jnp.concatenate([real_sum, imag_sum], axis=2).astype(jnp.bfloat16)

def reference(spectra, pair_blocks):
    whitened = whiten(spectra)
    lag_table = make_table()
    scaling = 1.0 / math.sqrt(WINDOWS * F)

    def correlate(pair_row):
        leading = lax.dynamic_slice_in_dim(whitened, (pair_row[0] * CH).astype(jnp.int32), CH, 2)
        trailing = lax.dynamic_slice_in_dim(whitened, (pair_row[1] * CH).astype(jnp.int32), CH, 2)
        cross = cross_spectrum(leading, trailing)
        result = jnp.dot(cross.reshape(CH * CH, 2 * F), lag_table, preferred_element_type=jnp.float32)
        return result.reshape(CH, CH, NLAG) * scaling
    return lax.map(correlate, pair_blocks)
```

```python
import functools
import math

import jax
import jax.numpy as jnp
from jax import lax
from jax.experimental import pallas as pl
from jax.experimental.pallas import tpu as pltpu
from jax.sharding import PartitionSpec as P

NLAG = 256
HALF_BAND = 64
MESH = pl.DeviceIdType.MESH

eps = 1e-05
first_bin = 60.0
samples = 15000.0

CORES = 2
TILE = 8
QUADS = 4


def smoothing(length_bins, half_width):
    indices = jnp.arange(length_bins, dtype=jnp.int32)
    return (jnp.abs(indices[:, None] - indices[None, :]) <= half_width).astype(jnp.float32)


def whiten(spectra):
    length_bins = spectra.shape[-1]
    real_part = spectra[0].astype(jnp.float32)
    imag_part = spectra[1].astype(jnp.float32)
    powers = real_part * real_part + imag_part * imag_part
    smoother = smoothing(length_bins, HALF_BAND)
    counts = jnp.sum(smoother, axis=0)
    rows_flat = powers.reshape(-1, length_bins)
    smooth = jnp.dot(rows_flat, smoother, precision=lax.Precision.HIGHEST) / counts
    factor = lax.rsqrt(smooth + eps).reshape(powers.shape)
    return jnp.stack([real_part * factor, imag_part * factor]).astype(jnp.bfloat16)


def make_table(length_bins):
    bin_freq = first_bin + jnp.arange(length_bins, dtype=jnp.float32)
    lag_steps = jnp.arange(NLAG, dtype=jnp.float32) - NLAG // 2
    angles = 2.0 * math.pi / samples * bin_freq[None, :] * lag_steps[:, None]
    return jnp.concatenate([jnp.cos(angles), -jnp.sin(angles)], axis=1).astype(jnp.bfloat16)


def arrange_kernel(x_ref, o_ref, turned):
    parts, channels, bins = x_ref.shape
    groups = bins // (QUADS * TILE)
    me = lax.rem(lax.axis_index("win"), QUADS)
    for part in range(parts):
        flipped = x_ref[part].astype(jnp.float32).T
        turned[part] = flipped.reshape(groups, QUADS, TILE, channels)

    def group_step(group, carry):
        rows = []
        for part in range(parts):
            for place in range(QUADS):
                quad = lax.rem(place - me + QUADS, QUADS)
                rows.append(turned[part, group, quad])
        o_ref[group] = jnp.concatenate(rows, axis=0).T.astype(o_ref.dtype)
        return carry

    lax.fori_loop(0, groups, group_step, 0, unroll=4)


def arrange(whitened):
    parts = whitened.shape[0] * whitened.shape[1]
    channels, bins = whitened.shape[2:]
    groups = bins // (QUADS * TILE)
    lanes = parts * QUADS * TILE
    return pl.pallas_call(
        arrange_kernel,
        out_shape=jax.ShapeDtypeStruct((groups, channels, lanes), jnp.bfloat16),
        in_specs=[pl.BlockSpec(memory_space=pltpu.VMEM)],
        out_specs=pl.BlockSpec(memory_space=pltpu.VMEM),
        scratch_shapes=[pltpu.VMEM((parts, groups, QUADS, TILE, channels), jnp.float32)],
        compiler_params=pltpu.CompilerParams(vmem_limit_bytes=24 * 2**20),
        name="arrange",
    )(whitened.reshape(parts, channels, bins))


def spread_kernel(reach, chans, wins, p_ref, o_ref, own_sem, s1, r1, s2, r2, s3, r3):
    chan = lax.axis_index("chan")
    win = lax.axis_index("win")
    row = win // CORES
    core = lax.rem(win, CORES)
    rows = wins // CORES
    other = row * CORES + (CORES - 1 - core)
    own = reach - 1
    offsets = list(range(1 - reach, reach + 1))
    order = sorted((o for o in offsets if o != 0), key=abs)

    def at(c):
        return lax.rem(c + chans, chans)

    def peer(step):
        return lax.rem(row + step + rows, rows) * CORES + core

    friends = sorted({o % chans for o in offsets if o} | {-o % chans for o in offsets if o})
    barrier = pltpu.get_barrier_semaphore()
    for f in friends:
        pl.semaphore_signal(barrier, inc=1, device_id=(at(chan + f), win), device_id_type=MESH)
    for step in range(1, rows):
        pl.semaphore_signal(barrier, inc=1, device_id=(chan, peer(step)), device_id_type=MESH)
    pl.semaphore_signal(barrier, inc=1, device_id=(chan, other), device_id_type=MESH)
    pl.semaphore_wait(barrier, len(friends) + rows)

    mine = pltpu.make_async_copy(p_ref, o_ref.at[own, win], own_sem)
    mine.start()

    def first(o):
        slot = o + own
        return pltpu.make_async_remote_copy(
            src_ref=p_ref, dst_ref=o_ref.at[slot, win], send_sem=s1.at[slot], recv_sem=r1.at[slot],
            device_id=(at(chan - o), win), device_id_type=MESH)

    def across(slot, step):
        src = p_ref if slot == own else o_ref.at[slot, win]
        return pltpu.make_async_remote_copy(
            src_ref=src, dst_ref=o_ref.at[slot, win], send_sem=s2.at[slot, step],
            recv_sem=r2.at[slot, step], device_id=(chan, peer(step)), device_id_type=MESH)

    def arrived(slot, step):
        place = o_ref.at[slot, peer(-step)]
        return pltpu.make_async_remote_copy(
            src_ref=place, dst_ref=place, send_sem=s2.at[slot, step],
            recv_sem=r2.at[slot, step], device_id=(chan, peer(step)), device_id_type=MESH)

    def beside(slot, step):
        piece = peer(-step) if step else win
        src = p_ref if (slot == own and not step) else o_ref.at[slot, piece]
        return pltpu.make_async_remote_copy(
            src_ref=src, dst_ref=o_ref.at[slot, piece], send_sem=s3.at[slot, step],
            recv_sem=r3.at[slot, step], device_id=(chan, other), device_id_type=MESH)

    def from_beside(slot, step):
        base = lax.rem(row - step + rows, rows) * CORES + (CORES - 1 - core)
        place = o_ref.at[slot, base]
        return pltpu.make_async_remote_copy(
            src_ref=place, dst_ref=place, send_sem=s3.at[slot, step],
            recv_sem=r3.at[slot, step], device_id=(chan, other), device_id_type=MESH)

    slots = [own] + [o + own for o in order]
    for o in order:
        first(o).start()
    for slot in slots:
        if slot != own:
            first(slot - own).wait_recv()
        for step in range(1, rows):
            across(slot, step).start()
        beside(slot, 0).start()
    for slot in slots:
        for step in range(1, rows):
            arrived(slot, step).wait_recv()
            beside(slot, step).start()
    for slot in slots:
        for step in range(rows):
            from_beside(slot, step).wait_recv()
    for slot in slots:
        if slot != own:
            first(slot - own).wait_send()
        for step in range(1, rows):
            across(slot, step).wait_send()
        for step in range(rows):
            beside(slot, step).wait_send()
    mine.wait()


def spread(piece, reach, chans, wins):
    slots = 2 * reach
    rows = wins // CORES
    dma = pltpu.SemaphoreType.DMA
    return pl.pallas_call(
        functools.partial(spread_kernel, reach, chans, wins),
        out_shape=jax.ShapeDtypeStruct((slots, wins) + piece.shape, piece.dtype),
        in_specs=[pl.BlockSpec(memory_space=pl.ANY)],
        out_specs=pl.BlockSpec(memory_space=pl.ANY),
        scratch_shapes=[dma, dma((slots,)), dma((slots,)), dma((slots, rows)), dma((slots, rows)),
                        dma((slots, rows)), dma((slots, rows))],
        compiler_params=pltpu.CompilerParams(collective_id=0, has_side_effects=True),
        name="spread",
    )(piece)


def correlate_kernel(first_steps, scaling, pick_ref, a_ref, b_ref, t_ref, o_ref, cross):
    step = pl.program_id(0)
    wins, chunk, channels, lanes = a_ref.shape[1:]
    half = channels // 2
    bins = cross.shape[2]

    @pl.when(step < first_steps)
    def _():
        lane = lax.broadcasted_iota(jnp.int32, (1, lanes), 1)
        place = (lane // TILE) % QUADS
        keep = lax.broadcasted_iota(jnp.int32, (TILE, lanes), 0) == lax.broadcasted_iota(
            jnp.int32, (TILE, lanes), 1) % TILE
        keep = keep.astype(jnp.float32)[None]
        sign = jnp.where(lane < lanes // 2, -1.0, 1.0)
        zero = jnp.zeros((channels, lanes), jnp.bfloat16)

        def merged(ref, group, bundle, quad):
            out = ref[0, bundle * QUADS, group].astype(jnp.float32)
            for m in range(1, QUADS):
                part = ref[0, bundle * QUADS + m, group].astype(jnp.float32)
                out = jnp.where(place == (m + quad) % QUADS, part, out)
            return out

        def spread_rows(x):
            wide = jnp.broadcast_to(x[:, None, :], (half, TILE, lanes)) * keep
            return wide.reshape(half * TILE, lanes).astype(jnp.bfloat16)

        for group in range(chunk):
            for pair in range(QUADS // 2):
                both = []
                for quad in (2 * pair, 2 * pair + 1):
                    total = None
                    for bundle in range(wins // QUADS):
                        a = merged(a_ref, group, bundle, quad)
                        b = merged(b_ref, group, bundle, quad)
                        bx = (pltpu.roll(b, lanes // 2, 1) * sign).astype(jnp.bfloat16)
                        b = b.astype(jnp.bfloat16)
                        left = jnp.concatenate([spread_rows(a[:half]), spread_rows(a[half:])], axis=1)
                        right = jnp.concatenate(
                            [jnp.concatenate([b, zero, bx, zero], axis=0),
                             jnp.concatenate([zero, b, zero, bx], axis=0)], axis=1)
                        prod = lax.dot_general(left, right, (((1,), (1,)), ((), ())),
                                               preferred_element_type=jnp.float32)
                        total = prod if total is None else total + prod
                    both.append(total.reshape(half, TILE, 4 * channels))
                tile = jnp.concatenate(both, axis=1).astype(jnp.bfloat16)
                start = pl.multiple_of((step * chunk + group) * QUADS * TILE + pair * 2 * TILE, 2 * TILE)
                cross[0, :, pl.ds(start, 2 * TILE), :] = tile[:, :, :2 * channels]
                cross[1, :, pl.ds(start, 2 * TILE), :] = tile[:, :, 2 * channels:]

    @pl.when(step >= first_steps)
    def _():
        count = o_ref.shape[1]
        base = (step - first_steps) * count
        for p in range(0, count, 2):
            total = None
            for part in range(2):
                wide = jnp.concatenate([cross[part, base + p], cross[part, base + p + 1]], axis=1)
                prod = jnp.dot(t_ref[:, part * bins:(part + 1) * bins], wide,
                               preferred_element_type=jnp.float32)
                total = prod if total is None else total + prod
            turned = (total * scaling).T
            for q in range(2):
                for h in range(2):
                    begin = (2 * q + h) * channels
                    o_ref[h, p + q] = turned[begin:begin + channels]


def correlate(picks, nearby, table, scaling):
    slots, wins, groups, channels, lanes = nearby.shape
    bins = groups * QUADS * TILE
    half = channels // 2
    chunk = 2
    per_step = 4
    first_steps = groups // chunk
    last_steps = half // per_step

    def source(which):
        return lambda s, pick: (pick[which], 0, jnp.minimum(s, first_steps - 1), 0, 0)

    block = (1, wins, chunk, channels, lanes)
    out = pl.pallas_call(
        functools.partial(correlate_kernel, first_steps, scaling),
        out_shape=jax.ShapeDtypeStruct((2, half, channels, NLAG), jnp.float32),
        grid_spec=pltpu.PrefetchScalarGridSpec(
            num_scalar_prefetch=1,
            grid=(first_steps + last_steps,),
            in_specs=[
                pl.BlockSpec(block, source(0)),
                pl.BlockSpec(block, source(1)),
                pl.BlockSpec((NLAG, 2 * bins), lambda s, pick: (0, 0)),
            ],
            out_specs=pl.BlockSpec(
                (2, per_step, channels, NLAG),
                lambda s, pick: (0, jnp.maximum(s - first_steps, 0), 0, 0)),
            scratch_shapes=[pltpu.VMEM((2, half, bins, 2 * channels), jnp.bfloat16)],
        ),
        compiler_params=pltpu.CompilerParams(
            dimension_semantics=("arbitrary",), vmem_limit_bytes=48 * 2**20),
        name="correlate",
    )(picks, nearby, nearby, table)
    return out.reshape(channels, channels, NLAG)


def per_device(chans, wins, spectra, pair_blocks):
    whitened = whiten(spectra)
    length_bins = spectra.shape[3]
    reach = pair_blocks.shape[0] * wins // 2
    table = make_table(length_bins)
    scaling = 1.0 / math.sqrt(spectra.shape[1] * wins * length_bins)
    base_block = lax.axis_index("chan") - (reach - 1)
    picks = jnp.mod(pair_blocks - base_block, chans)
    nearby = spread(arrange(whitened), reach, chans, wins)
    rows = [correlate(picks[r], nearby, table, scaling) for r in range(pair_blocks.shape[0])]
    return jnp.stack(rows)


def solution(mesh):
    in_specs = (P(None, "win", "chan", None), P(("chan", "win"), None))
    out_specs = P(("chan", "win"), None, None, None)
    return jax.shard_map(
        functools.partial(per_device, mesh.shape["chan"], mesh.shape["win"]),
        mesh=mesh, in_specs=in_specs, out_specs=out_specs, check_vma=False
    )
```

```python
import functools
import math

import jax
import jax.numpy as jnp
import ml_dtypes
import numpy as np
from jax import lax
from jax.experimental import pallas as pl
from jax.experimental.pallas import tpu as pltpu
from jax.sharding import PartitionSpec as P

NLAG = 256
HALF_BAND = 64
MESH = pl.DeviceIdType.MESH

eps = 1e-05
first_bin = 60.0
samples = 15000.0

CORES = 2
TILE = 8
QUADS = 4


def smoothing(length_bins, half_width):
    indices = jnp.arange(length_bins, dtype=jnp.int32)
    return (jnp.abs(indices[:, None] - indices[None, :]) <= half_width).astype(jnp.float32)


def whiten(spectra):
    length_bins = spectra.shape[-1]
    real_part = spectra[0].astype(jnp.float32)
    imag_part = spectra[1].astype(jnp.float32)
    powers = real_part * real_part + imag_part * imag_part
    smoother = smoothing(length_bins, HALF_BAND)
    counts = jnp.sum(smoother, axis=0)
    rows_flat = powers.reshape(-1, length_bins)
    smooth = jnp.dot(rows_flat, smoother, precision=lax.Precision.HIGHEST) / counts
    factor = lax.rsqrt(smooth + eps).reshape(powers.shape)
    return jnp.stack([real_part * factor, imag_part * factor]).astype(jnp.bfloat16)


def make_table(length_bins):
    bin_freq = np.float32(first_bin) + np.arange(length_bins, dtype=np.float32)
    lag_steps = np.arange(NLAG, dtype=np.float32) - np.float32(NLAG // 2)
    angles = np.float32(2.0 * math.pi / samples) * bin_freq[None, :] * lag_steps[:, None]
    return np.concatenate([np.cos(angles), -np.sin(angles)], axis=1).astype(ml_dtypes.bfloat16)


def arrange_kernel(x_ref, o_ref, turned):
    parts, channels, bins = x_ref.shape
    groups = bins // (QUADS * TILE)
    me = lax.rem(lax.axis_index("win"), QUADS)
    for part in range(parts):
        flipped = x_ref[part].astype(jnp.float32).T
        turned[part] = flipped.reshape(groups, QUADS, TILE, channels)

    def group_step(group, carry):
        rows = []
        for part in range(parts):
            for place in range(QUADS):
                quad = lax.rem(place - me + QUADS, QUADS)
                rows.append(turned[part, group, quad])
        o_ref[group] = jnp.concatenate(rows, axis=0).T.astype(o_ref.dtype)
        return carry

    lax.fori_loop(0, groups, group_step, 0, unroll=4)


def arrange(whitened):
    parts = whitened.shape[0] * whitened.shape[1]
    channels, bins = whitened.shape[2:]
    groups = bins // (QUADS * TILE)
    lanes = parts * QUADS * TILE
    return pl.pallas_call(
        arrange_kernel,
        out_shape=jax.ShapeDtypeStruct((groups, channels, lanes), jnp.bfloat16),
        in_specs=[pl.BlockSpec(memory_space=pltpu.VMEM)],
        out_specs=pl.BlockSpec(memory_space=pltpu.VMEM),
        scratch_shapes=[pltpu.VMEM((parts, groups, QUADS, TILE, channels), jnp.float32)],
        compiler_params=pltpu.CompilerParams(vmem_limit_bytes=24 * 2**20),
        name="arrange",
    )(whitened.reshape(parts, channels, bins))


def spread_kernel(reach, chans, wins, chunks, p_ref, o_ref, own_sem, s1, r1, s2, r2, s3, r3):
    chan = lax.axis_index("chan")
    win = lax.axis_index("win")
    row = win // CORES
    core = lax.rem(win, CORES)
    rows = wins // CORES
    other = row * CORES + (CORES - 1 - core)
    own = reach - 1
    size = p_ref.shape[0] // chunks
    offsets = list(range(1 - reach, reach + 1))
    order = sorted((o for o in offsets if o != 0), key=abs)

    def at(c):
        return lax.rem(c + chans, chans)

    def peer(step):
        return lax.rem(row + step + rows, rows) * CORES + core

    friends = sorted({o % chans for o in offsets if o} | {-o % chans for o in offsets if o})
    barrier = pltpu.get_barrier_semaphore()
    for f in friends:
        pl.semaphore_signal(barrier, inc=1, device_id=(at(chan + f), win), device_id_type=MESH)
    for step in range(1, rows):
        pl.semaphore_signal(barrier, inc=1, device_id=(chan, peer(step)), device_id_type=MESH)
    pl.semaphore_signal(barrier, inc=1, device_id=(chan, other), device_id_type=MESH)
    pl.semaphore_wait(barrier, len(friends) + rows)

    mine = pltpu.make_async_copy(p_ref, o_ref.at[own, win], own_sem)
    mine.start()

    def place(slot, piece, ch):
        return o_ref.at[slot, piece, pl.ds(ch * size, size)]

    def origin(slot, step, ch):
        if slot == own and step == 0:
            return p_ref.at[pl.ds(ch * size, size)]
        return place(slot, peer(-step), ch)

    def whole_way(o, ch):
        return abs(o) == 1 and ch % 2 == 0

    def along(o, step, ch):
        slot = o + own
        return pltpu.make_async_remote_copy(
            src_ref=origin(own, step, ch), dst_ref=place(slot, peer(-step), ch),
            send_sem=s1.at[slot, step, ch], recv_sem=r1.at[slot, step, ch],
            device_id=(at(chan - o), win), device_id_type=MESH)

    def across(slot, step, ch):
        return pltpu.make_async_remote_copy(
            src_ref=origin(slot, 0, ch), dst_ref=place(slot, win, ch),
            send_sem=s2.at[slot, step, ch], recv_sem=r2.at[slot, step, ch],
            device_id=(chan, peer(step)), device_id_type=MESH)

    def arrived(slot, step, ch):
        here = place(slot, peer(-step), ch)
        return pltpu.make_async_remote_copy(
            src_ref=here, dst_ref=here, send_sem=s2.at[slot, step, ch],
            recv_sem=r2.at[slot, step, ch], device_id=(chan, peer(step)), device_id_type=MESH)

    def beside(slot, step, ch):
        return pltpu.make_async_remote_copy(
            src_ref=origin(slot, step, ch), dst_ref=place(slot, peer(-step), ch),
            send_sem=s3.at[slot, step, ch], recv_sem=r3.at[slot, step, ch],
            device_id=(chan, other), device_id_type=MESH)

    def from_beside(slot, step, ch):
        base = lax.rem(row - step + rows, rows) * CORES + (CORES - 1 - core)
        here = place(slot, base, ch)
        return pltpu.make_async_remote_copy(
            src_ref=here, dst_ref=here, send_sem=s3.at[slot, step, ch],
            recv_sem=r3.at[slot, step, ch], device_id=(chan, other), device_id_type=MESH)

    steps = range(1, rows)
    for ch in range(chunks):
        for step in steps:
            across(own, step, ch).start()
        for o in order:
            along(o, 0, ch).start()
        beside(own, 0, ch).start()

    def second(ch):
        for step in steps:
            arrived(own, step, ch).wait_recv()
            for o in order:
                if whole_way(o, ch):
                    along(o, step, ch).start()
            beside(own, step, ch).start()
        for o in order:
            along(o, 0, ch).wait_recv()
            if not whole_way(o, ch):
                for step in steps:
                    across(o + own, step, ch).start()
            beside(o + own, 0, ch).start()

    def third(ch):
        for o in order:
            for step in steps:
                if whole_way(o, ch):
                    along(o, step, ch).wait_recv()
                else:
                    arrived(o + own, step, ch).wait_recv()
                beside(o + own, step, ch).start()

    for ch in range(chunks + 1):
        if ch < chunks:
            second(ch)
        if ch > 0:
            third(ch - 1)
    for ch in range(chunks):
        for o in offsets:
            for step in range(rows):
                from_beside(o + own, step, ch).wait_recv()
    for ch in range(chunks):
        for o in offsets:
            for step in range(rows):
                if o != 0 and (step == 0 or whole_way(o, ch)):
                    along(o, step, ch).wait_send()
                if step > 0 and (o == 0 or not whole_way(o, ch)):
                    across(o + own, step, ch).wait_send()
                beside(o + own, step, ch).wait_send()
    mine.wait()


def spread(piece, reach, chans, wins):
    slots = 2 * reach
    rows = wins // CORES
    chunks = 4 if rows <= 2 else 2
    sems = pltpu.SemaphoreType.DMA((slots, rows, chunks))
    return pl.pallas_call(
        functools.partial(spread_kernel, reach, chans, wins, chunks),
        out_shape=jax.ShapeDtypeStruct((slots, wins) + piece.shape, piece.dtype),
        in_specs=[pl.BlockSpec(memory_space=pl.ANY)],
        out_specs=pl.BlockSpec(memory_space=pl.ANY),
        scratch_shapes=[pltpu.SemaphoreType.DMA] + [sems] * 6,
        compiler_params=pltpu.CompilerParams(collective_id=0, has_side_effects=True),
        name="spread",
    )(piece)


def correlate_kernel(first_steps, scaling, pick_ref, a_ref, b_ref, t_ref, o_ref, cross):
    step = pl.program_id(0)
    wins, chunk, channels, lanes = a_ref.shape[1:]
    half = channels // 2
    bins = cross.shape[2]

    @pl.when(step < first_steps)
    def _():
        lane = lax.broadcasted_iota(jnp.int32, (1, lanes), 1)
        place = (lane // TILE) % QUADS
        keep = lax.broadcasted_iota(jnp.int32, (TILE, lanes), 0) == lax.broadcasted_iota(
            jnp.int32, (TILE, lanes), 1) % TILE
        keep = keep.astype(jnp.float32)[None]
        sign = jnp.where(lane < lanes // 2, -1.0, 1.0)
        zero = jnp.zeros((channels, lanes), jnp.bfloat16)

        def merged(ref, group, bundle, quad):
            out = ref[0, bundle * QUADS, group].astype(jnp.float32)
            for m in range(1, QUADS):
                part = ref[0, bundle * QUADS + m, group].astype(jnp.float32)
                out = jnp.where(place == (m + quad) % QUADS, part, out)
            return out

        def spread_rows(x):
            wide = jnp.broadcast_to(x[:, None, :], (half, TILE, lanes)) * keep
            return wide.reshape(half * TILE, lanes).astype(jnp.bfloat16)

        for group in range(chunk):
            for pair in range(QUADS // 2):
                both = []
                for quad in (2 * pair, 2 * pair + 1):
                    total = None
                    for bundle in range(wins // QUADS):
                        a = merged(a_ref, group, bundle, quad)
                        b = merged(b_ref, group, bundle, quad)
                        bx = (pltpu.roll(b, lanes // 2, 1) * sign).astype(jnp.bfloat16)
                        b = b.astype(jnp.bfloat16)
                        left = jnp.concatenate([spread_rows(a[:half]), spread_rows(a[half:])], axis=1)
                        right = jnp.concatenate(
                            [jnp.concatenate([b, zero, bx, zero], axis=0),
                             jnp.concatenate([zero, b, zero, bx], axis=0)], axis=1)
                        prod = lax.dot_general(left, right, (((1,), (1,)), ((), ())),
                                               preferred_element_type=jnp.float32)
                        total = prod if total is None else total + prod
                    both.append(total.reshape(half, TILE, 4 * channels))
                tile = jnp.concatenate(both, axis=1).astype(jnp.bfloat16)
                start = pl.multiple_of((step * chunk + group) * QUADS * TILE + pair * 2 * TILE, 2 * TILE)
                cross[0, :, pl.ds(start, 2 * TILE), :] = tile[:, :, :2 * channels]
                cross[1, :, pl.ds(start, 2 * TILE), :] = tile[:, :, 2 * channels:]

    @pl.when(step >= first_steps)
    def _():
        count = o_ref.shape[1]
        base = (step - first_steps) * count
        for p in range(0, count, 2):
            total = None
            for part in range(2):
                wide = jnp.concatenate([cross[part, base + p], cross[part, base + p + 1]], axis=1)
                prod = jnp.dot(t_ref[:, part * bins:(part + 1) * bins], wide,
                               preferred_element_type=jnp.float32)
                total = prod if total is None else total + prod
            turned = (total * scaling).T
            for q in range(2):
                for h in range(2):
                    begin = (2 * q + h) * channels
                    o_ref[h, p + q] = turned[begin:begin + channels]


def correlate(picks, nearby, table, scaling):
    slots, wins, groups, channels, lanes = nearby.shape
    bins = groups * QUADS * TILE
    half = channels // 2
    chunk = 2
    per_step = 4
    first_steps = groups // chunk
    last_steps = half // per_step

    def source(which):
        return lambda s, pick: (pick[which], 0, jnp.minimum(s, first_steps - 1), 0, 0)

    block = (1, wins, chunk, channels, lanes)
    out = pl.pallas_call(
        functools.partial(correlate_kernel, first_steps, scaling),
        out_shape=jax.ShapeDtypeStruct((2, half, channels, NLAG), jnp.float32),
        grid_spec=pltpu.PrefetchScalarGridSpec(
            num_scalar_prefetch=1,
            grid=(first_steps + last_steps,),
            in_specs=[
                pl.BlockSpec(block, source(0)),
                pl.BlockSpec(block, source(1)),
                pl.BlockSpec((NLAG, 2 * bins), lambda s, pick: (0, 0)),
            ],
            out_specs=pl.BlockSpec(
                (2, per_step, channels, NLAG),
                lambda s, pick: (0, jnp.maximum(s - first_steps, 0), 0, 0)),
            scratch_shapes=[pltpu.VMEM((2, half, bins, 2 * channels), jnp.bfloat16)],
        ),
        compiler_params=pltpu.CompilerParams(
            dimension_semantics=("arbitrary",), vmem_limit_bytes=48 * 2**20),
        name="correlate",
    )(picks, nearby, nearby, table)
    return out.reshape(channels, channels, NLAG)


def per_device(chans, wins, spectra, pair_blocks):
    whitened = whiten(spectra)
    length_bins = spectra.shape[3]
    reach = pair_blocks.shape[0] * wins // 2
    table = jnp.asarray(make_table(length_bins))
    scaling = 1.0 / math.sqrt(spectra.shape[1] * wins * length_bins)
    base_block = lax.axis_index("chan") - (reach - 1)
    picks = jnp.mod(pair_blocks - base_block, chans)
    nearby = spread(arrange(whitened), reach, chans, wins)
    rows = [correlate(picks[r], nearby, table, scaling) for r in range(pair_blocks.shape[0])]
    return jnp.stack(rows)


def solution(mesh):
    in_specs = (P(None, "win", "chan", None), P(("chan", "win"), None))
    out_specs = P(("chan", "win"), None, None, None)
    return jax.shard_map(
        functools.partial(per_device, mesh.shape["chan"], mesh.shape["win"]),
        mesh=mesh, in_specs=in_specs, out_specs=out_specs, check_vma=False
    )
```

```python
import functools
import math

import jax
import jax.numpy as jnp
import ml_dtypes
import numpy as np
from jax import lax
from jax.experimental import pallas as pl
from jax.experimental.pallas import tpu as pltpu
from jax.sharding import PartitionSpec as P

NLAG = 256
HALF_BAND = 64
MESH = pl.DeviceIdType.MESH

eps = 1e-05
first_bin = 60.0
samples = 15000.0

CORES = 2
TILE = 8
QUADS = 4


def smoothing(length_bins, half_width):
    indices = jnp.arange(length_bins, dtype=jnp.int32)
    return (jnp.abs(indices[:, None] - indices[None, :]) <= half_width).astype(jnp.float32)


def whiten(spectra):
    length_bins = spectra.shape[-1]
    real_part = spectra[0].astype(jnp.float32)
    imag_part = spectra[1].astype(jnp.float32)
    powers = real_part * real_part + imag_part * imag_part
    smoother = smoothing(length_bins, HALF_BAND)
    counts = jnp.sum(smoother, axis=0)
    rows_flat = powers.reshape(-1, length_bins)
    smooth = jnp.dot(rows_flat, smoother, precision=lax.Precision.HIGHEST) / counts
    factor = lax.rsqrt(smooth + eps).reshape(powers.shape)
    return jnp.stack([real_part * factor, imag_part * factor]).astype(jnp.bfloat16)


def make_table(length_bins):
    bin_freq = np.float32(first_bin) + np.arange(length_bins, dtype=np.float32)
    lag_steps = np.arange(NLAG, dtype=np.float32) - np.float32(NLAG // 2)
    angles = np.float32(2.0 * math.pi / samples) * bin_freq[None, :] * lag_steps[:, None]
    return np.concatenate([np.cos(angles), -np.sin(angles)], axis=1).astype(ml_dtypes.bfloat16)


def arrange_kernel(x_ref, o_ref, turned):
    parts, channels, bins = x_ref.shape
    groups = bins // (QUADS * TILE)
    me = lax.rem(lax.axis_index("win"), QUADS)
    for part in range(parts):
        flipped = x_ref[part].astype(jnp.float32).T
        turned[part] = flipped.reshape(groups, QUADS, TILE, channels)

    def group_step(group, carry):
        rows = []
        for part in range(parts):
            for place in range(QUADS):
                quad = lax.rem(place - me + QUADS, QUADS)
                rows.append(turned[part, group, quad])
        o_ref[group] = jnp.concatenate(rows, axis=0).T.astype(o_ref.dtype)
        return carry

    lax.fori_loop(0, groups, group_step, 0, unroll=4)


def arrange(whitened):
    parts = whitened.shape[0] * whitened.shape[1]
    channels, bins = whitened.shape[2:]
    groups = bins // (QUADS * TILE)
    lanes = parts * QUADS * TILE
    return pl.pallas_call(
        arrange_kernel,
        out_shape=jax.ShapeDtypeStruct((groups, channels, lanes), jnp.bfloat16),
        in_specs=[pl.BlockSpec(memory_space=pltpu.VMEM)],
        out_specs=pl.BlockSpec(memory_space=pltpu.VMEM),
        scratch_shapes=[pltpu.VMEM((parts, groups, QUADS, TILE, channels), jnp.float32)],
        compiler_params=pltpu.CompilerParams(vmem_limit_bytes=24 * 2**20),
        name="arrange",
    )(whitened.reshape(parts, channels, bins))


def cross_chunk(pick, buf, cross):
    _, wins, groups, channels, lanes = buf.shape
    half = channels // 2
    lane = lax.broadcasted_iota(jnp.int32, (1, lanes), 1)
    place = (lane // TILE) % QUADS
    keep = lax.broadcasted_iota(jnp.int32, (TILE, lanes), 0) == lax.broadcasted_iota(
        jnp.int32, (TILE, lanes), 1) % TILE
    keep = keep.astype(jnp.float32)[None]
    sign = jnp.where(lane < lanes // 2, -1.0, 1.0)
    zero = jnp.zeros((channels, lanes), jnp.bfloat16)

    def merged(pieces, quad):
        out = pieces[0]
        for m in range(1, QUADS):
            out = jnp.where(place == (m + quad) % QUADS, pieces[m], out)
        return out

    def spread_rows(x):
        wide = jnp.broadcast_to(x[:, None, :], (half, TILE, lanes)) * keep
        return wide.reshape(half * TILE, lanes).astype(jnp.bfloat16)

    def group_step(group, carry):
        a_pieces = [buf[pick[0], m, group].astype(jnp.float32) for m in range(wins)]
        b_pieces = [buf[pick[1], m, group].astype(jnp.float32) for m in range(wins)]
        for pair in range(QUADS // 2):
            both = []
            for quad in (2 * pair, 2 * pair + 1):
                total = None
                for bundle in range(0, wins, QUADS):
                    a = merged(a_pieces[bundle:bundle + QUADS], quad)
                    b = merged(b_pieces[bundle:bundle + QUADS], quad)
                    bx = (pltpu.roll(b, lanes // 2, 1) * sign).astype(jnp.bfloat16)
                    b = b.astype(jnp.bfloat16)
                    left = jnp.concatenate([spread_rows(a[:half]), spread_rows(a[half:])], axis=1)
                    right = jnp.concatenate(
                        [jnp.concatenate([b, zero, bx, zero], axis=0),
                         jnp.concatenate([zero, b, zero, bx], axis=0)], axis=1)
                    prod = lax.dot_general(left, right, (((1,), (1,)), ((), ())),
                                           preferred_element_type=jnp.float32)
                    total = prod if total is None else total + prod
                both.append(total.reshape(half, TILE, 4 * channels))
            tile = jnp.concatenate(both, axis=1).astype(jnp.bfloat16)
            start = pl.multiple_of(group * (QUADS * TILE) + pair * 2 * TILE, 2 * TILE)
            cross[0, :, pl.ds(start, 2 * TILE), :] = tile[:, :, :2 * channels]
            cross[1, :, pl.ds(start, 2 * TILE), :] = tile[:, :, 2 * channels:]
        return carry

    lax.fori_loop(0, groups, group_step, 0, unroll=2)


def lag_chunk(begin, bins, t_ref, cross, o_ref):
    size = cross.shape[2]

    def pair_step(p, carry):
        total = None
        for part in range(2):
            wide = jnp.concatenate([cross[part, 2 * p], cross[part, 2 * p + 1]], axis=1)
            first = part * bins + begin
            prod = jnp.dot(t_ref[:, first:first + size], wide, preferred_element_type=jnp.float32)
            total = prod if total is None else total + prod
        if begin:
            total = total + o_ref[p]
        o_ref[p] = total
        return carry

    lax.fori_loop(0, o_ref.shape[0], pair_step, 0, unroll=2)


def spread_kernel(reach, chans, wins, chunks, pair_ref, p_ref, t_ref, o_ref, cross, own_sem,
                  s1, r1, s2, r2, s3, r3, *bufs):
    chan = lax.axis_index("chan")
    win = lax.axis_index("win")
    row = win // CORES
    core = lax.rem(win, CORES)
    rows = wins // CORES
    other = row * CORES + (CORES - 1 - core)
    own = reach - 1
    size = p_ref.shape[0] // chunks
    offsets = list(range(1 - reach, reach + 1))
    order = sorted((o for o in offsets if o != 0), key=abs)

    def at(c):
        return lax.rem(c + chans, chans)

    def peer(step):
        return lax.rem(row + step + rows, rows) * CORES + core

    friends = sorted({o % chans for o in offsets if o} | {-o % chans for o in offsets if o})
    barrier = pltpu.get_barrier_semaphore()
    for f in friends:
        pl.semaphore_signal(barrier, inc=1, device_id=(at(chan + f), win), device_id_type=MESH)
    for step in range(1, rows):
        pl.semaphore_signal(barrier, inc=1, device_id=(chan, peer(step)), device_id_type=MESH)
    pl.semaphore_signal(barrier, inc=1, device_id=(chan, other), device_id_type=MESH)
    pl.semaphore_wait(barrier, len(friends) + rows)

    def mine(ch):
        return pltpu.make_async_copy(origin(own, 0, ch), place(own, win, ch), own_sem.at[ch])

    def place(slot, piece, ch):
        return bufs[ch].at[slot, piece]

    def origin(slot, step, ch):
        if slot == own and step == 0:
            return p_ref.at[pl.ds(ch * size, size)]
        return place(slot, peer(-step), ch)

    def whole_way(o, ch):
        return abs(o) == 1 and ch % 2 == 0

    def along(o, step, ch):
        slot = o + own
        return pltpu.make_async_remote_copy(
            src_ref=origin(own, step, ch), dst_ref=place(slot, peer(-step), ch),
            send_sem=s1.at[slot, step, ch], recv_sem=r1.at[slot, step, ch],
            device_id=(at(chan - o), win), device_id_type=MESH)

    def across(slot, step, ch):
        return pltpu.make_async_remote_copy(
            src_ref=origin(slot, 0, ch), dst_ref=place(slot, win, ch),
            send_sem=s2.at[slot, step, ch], recv_sem=r2.at[slot, step, ch],
            device_id=(chan, peer(step)), device_id_type=MESH)

    def arrived(slot, step, ch):
        here = place(slot, peer(-step), ch)
        return pltpu.make_async_remote_copy(
            src_ref=here, dst_ref=here, send_sem=s2.at[slot, step, ch],
            recv_sem=r2.at[slot, step, ch], device_id=(chan, peer(step)), device_id_type=MESH)

    def beside(slot, step, ch):
        return pltpu.make_async_remote_copy(
            src_ref=origin(slot, step, ch), dst_ref=place(slot, peer(-step), ch),
            send_sem=s3.at[slot, step, ch], recv_sem=r3.at[slot, step, ch],
            device_id=(chan, other), device_id_type=MESH)

    def from_beside(slot, step, ch):
        base = lax.rem(row - step + rows, rows) * CORES + (CORES - 1 - core)
        here = place(slot, base, ch)
        return pltpu.make_async_remote_copy(
            src_ref=here, dst_ref=here, send_sem=s3.at[slot, step, ch],
            recv_sem=r3.at[slot, step, ch], device_id=(chan, other), device_id_type=MESH)

    steps = range(1, rows)
    for ch in range(chunks):
        for step in steps:
            across(own, step, ch).start()
        for o in order:
            along(o, 0, ch).start()
        beside(own, 0, ch).start()
        mine(ch).start()

    def second(ch):
        for step in steps:
            arrived(own, step, ch).wait_recv()
            for o in order:
                if whole_way(o, ch):
                    along(o, step, ch).start()
            beside(own, step, ch).start()
        for o in order:
            along(o, 0, ch).wait_recv()
            if not whole_way(o, ch):
                for step in steps:
                    across(o + own, step, ch).start()
            beside(o + own, 0, ch).start()

    def third(ch):
        for o in order:
            for step in steps:
                if whole_way(o, ch):
                    along(o, step, ch).wait_recv()
                else:
                    arrived(o + own, step, ch).wait_recv()
                beside(o + own, step, ch).start()

    pick = [jnp.minimum(lax.rem(pair_ref[0, n] - (chan - own) + 2 * chans, chans), 2 * reach - 1)
            for n in range(2)]
    bins = t_ref.shape[1] // 2

    def compute(ch):
        mine(ch).wait()
        for o in offsets:
            for step in range(rows):
                from_beside(o + own, step, ch).wait_recv()
        cross_chunk(pick, bufs[ch], cross)
        lag_chunk(ch * (bins // chunks), bins, t_ref, cross, o_ref)

    for ch in range(chunks + 2):
        if ch < chunks:
            second(ch)
        if 0 <= ch - 1 < chunks:
            third(ch - 1)
        if ch - 2 >= 0:
            compute(ch - 2)
    for ch in range(chunks):
        for o in offsets:
            for step in range(rows):
                if o != 0 and (step == 0 or whole_way(o, ch)):
                    along(o, step, ch).wait_send()
                if step > 0 and (o == 0 or not whole_way(o, ch)):
                    across(o + own, step, ch).wait_send()
                beside(o + own, step, ch).wait_send()


def spread(pairs, piece, table, reach, chans, wins):
    slots = 2 * reach
    rows = wins // CORES
    chunks = 4
    groups, channels, lanes = piece.shape
    lags, bins = table.shape[0], table.shape[1] // 2
    half = channels // 2
    size = groups // chunks
    sems = pltpu.SemaphoreType.DMA((slots, rows, chunks))
    buf = pltpu.VMEM((slots, wins, size, channels, lanes), piece.dtype)
    vmem = pl.BlockSpec(memory_space=pltpu.VMEM)
    return pl.pallas_call(
        functools.partial(spread_kernel, reach, chans, wins, chunks),
        out_shape=jax.ShapeDtypeStruct((half // 2, lags, 4 * channels), jnp.float32),
        in_specs=[pl.BlockSpec(memory_space=pltpu.SMEM), vmem, vmem],
        out_specs=vmem,
        scratch_shapes=[pltpu.VMEM((2, half, bins // chunks, 2 * channels), jnp.bfloat16),
                        pltpu.SemaphoreType.DMA((chunks,))] + [sems] * 6 + [buf] * chunks,
        compiler_params=pltpu.CompilerParams(
            collective_id=0, has_side_effects=True, vmem_limit_bytes=56 * 2**20),
        name="spread",
    )(pairs, piece, table)


def finish_kernel(scaling, x_ref, o_ref):
    channels = o_ref.shape[2]
    for p in range(x_ref.shape[0]):
        turned = (x_ref[p] * scaling).T
        for q in range(2):
            for h in range(2):
                begin = (2 * q + h) * channels
                o_ref[h, 2 * p + q] = turned[begin:begin + channels]


def finish(sums, scaling):
    count, lags, width = sums.shape
    channels = width // 4
    per_step = 2
    out = pl.pallas_call(
        functools.partial(finish_kernel, scaling),
        out_shape=jax.ShapeDtypeStruct((2, 2 * count, channels, lags), jnp.float32),
        grid=(count // per_step,),
        in_specs=[pl.BlockSpec((per_step, lags, width), lambda s: (s, 0, 0))],
        out_specs=pl.BlockSpec((2, 2 * per_step, channels, lags), lambda s: (0, s, 0, 0)),
        compiler_params=pltpu.CompilerParams(vmem_limit_bytes=24 * 2**20),
        name="finish",
    )(sums)
    return out.reshape(1, channels, channels, lags)


def per_device(chans, wins, spectra, pair_blocks):
    whitened = whiten(spectra)
    length_bins = spectra.shape[3]
    reach = pair_blocks.shape[0] * wins // 2
    table = jnp.asarray(make_table(length_bins))
    scaling = 1.0 / math.sqrt(spectra.shape[1] * wins * length_bins)
    return finish(spread(pair_blocks, arrange(whitened), table, reach, chans, wins), scaling)


def solution(mesh):
    in_specs = (P(None, "win", "chan", None), P(("chan", "win"), None))
    out_specs = P(("chan", "win"), None, None, None)
    return jax.shard_map(
        functools.partial(per_device, mesh.shape["chan"], mesh.shape["win"]),
        mesh=mesh, in_specs=in_specs, out_specs=out_specs, check_vma=False
    )
```

```python
import functools
import math

import jax
import jax.numpy as jnp
import ml_dtypes
import numpy as np
from jax import lax
from jax.experimental import pallas as pl
from jax.experimental.pallas import tpu as pltpu
from jax.sharding import PartitionSpec as P

NLAG = 256
HALF_BAND = 64
MESH = pl.DeviceIdType.MESH

eps = 1e-05
first_bin = 60.0
samples = 15000.0

CORES = 2
TILE = 8
QUADS = 4


def smoothing(length_bins, half_width):
    indices = jnp.arange(length_bins, dtype=jnp.int32)
    return (jnp.abs(indices[:, None] - indices[None, :]) <= half_width).astype(jnp.float32)


def whiten(spectra):
    length_bins = spectra.shape[-1]
    real_part = spectra[0].astype(jnp.float32)
    imag_part = spectra[1].astype(jnp.float32)
    powers = real_part * real_part + imag_part * imag_part
    smoother = smoothing(length_bins, HALF_BAND)
    counts = jnp.sum(smoother, axis=0)
    rows_flat = powers.reshape(-1, length_bins)
    smooth = jnp.dot(rows_flat, smoother, precision=lax.Precision.HIGHEST) / counts
    factor = lax.rsqrt(smooth + eps).reshape(powers.shape)
    return jnp.stack([real_part * factor, imag_part * factor]).astype(jnp.bfloat16)


def make_table(length_bins):
    bin_freq = np.float32(first_bin) + np.arange(length_bins, dtype=np.float32)
    lag_steps = np.arange(NLAG, dtype=np.float32) - np.float32(NLAG // 2)
    angles = np.float32(2.0 * math.pi / samples) * bin_freq[None, :] * lag_steps[:, None]
    return np.concatenate([np.cos(angles), -np.sin(angles)], axis=1).astype(ml_dtypes.bfloat16)


def arrange_kernel(x_ref, o_ref, turned):
    parts, channels, bins = x_ref.shape
    groups = bins // (QUADS * TILE)
    me = lax.rem(lax.axis_index("win"), QUADS)
    for part in range(parts):
        flipped = x_ref[part].astype(jnp.float32).T
        turned[part] = flipped.reshape(groups, QUADS, TILE, channels)

    def group_step(group, carry):
        rows = []
        for part in range(parts):
            for place in range(QUADS):
                quad = lax.rem(place - me + QUADS, QUADS)
                rows.append(turned[part, group, quad])
        o_ref[group] = jnp.concatenate(rows, axis=0).T.astype(o_ref.dtype)
        return carry

    lax.fori_loop(0, groups, group_step, 0, unroll=4)


def arrange(whitened):
    parts = whitened.shape[0] * whitened.shape[1]
    channels, bins = whitened.shape[2:]
    groups = bins // (QUADS * TILE)
    lanes = parts * QUADS * TILE
    return pl.pallas_call(
        arrange_kernel,
        out_shape=jax.ShapeDtypeStruct((groups, channels, lanes), jnp.bfloat16),
        in_specs=[pl.BlockSpec(memory_space=pltpu.VMEM)],
        out_specs=pl.BlockSpec(memory_space=pltpu.VMEM),
        scratch_shapes=[pltpu.VMEM((parts, groups, QUADS, TILE, channels), jnp.float32)],
        compiler_params=pltpu.CompilerParams(vmem_limit_bytes=24 * 2**20),
        name="arrange",
    )(whitened.reshape(parts, channels, bins))


def cross_chunk(pick, buf, cross):
    _, wins, groups, channels, lanes = buf.shape
    half = channels // 2
    lane = lax.broadcasted_iota(jnp.int32, (1, lanes), 1)
    place = (lane // TILE) % QUADS
    keep = lax.broadcasted_iota(jnp.int32, (2 * TILE, lanes), 0) % TILE == lax.broadcasted_iota(
        jnp.int32, (2 * TILE, lanes), 1) % TILE
    keep = keep.astype(jnp.float32).astype(jnp.bfloat16)[None]
    sign = jnp.where(lane < lanes // 2, -1.0, 1.0)
    zero = jnp.zeros((channels, lanes), jnp.bfloat16)

    def merged(pieces, quad):
        out = pieces[0]
        for m in range(1, QUADS):
            out = jnp.where(place == (m + quad) % QUADS, pieces[m], out)
        return out

    def spread_rows(x):
        wide = jnp.broadcast_to(x[:, None, :], (half, TILE, lanes))
        wide = wide.reshape(half * TILE // (2 * TILE), 2 * TILE, lanes).astype(jnp.bfloat16) * keep
        return wide.reshape(half * TILE, lanes)

    def group_step(group, carry):
        a_pieces = [buf[pick[0], m, group].astype(jnp.float32) for m in range(wins)]
        b_pieces = [buf[pick[1], m, group].astype(jnp.float32) for m in range(wins)]
        for pair in range(QUADS // 2):
            both = []
            for quad in (2 * pair, 2 * pair + 1):
                total = None
                for bundle in range(0, wins, QUADS):
                    a = merged(a_pieces[bundle:bundle + QUADS], quad)
                    b = merged(b_pieces[bundle:bundle + QUADS], quad)
                    bx = (pltpu.roll(b, lanes // 2, 1) * sign).astype(jnp.bfloat16)
                    b = b.astype(jnp.bfloat16)
                    left = jnp.concatenate([spread_rows(a[:half]), spread_rows(a[half:])], axis=1)
                    right = jnp.concatenate(
                        [jnp.concatenate([b, zero, bx, zero], axis=0),
                         jnp.concatenate([zero, b, zero, bx], axis=0)], axis=1)
                    prod = lax.dot_general(left, right, (((1,), (1,)), ((), ())),
                                           preferred_element_type=jnp.float32)
                    total = prod if total is None else total + prod
                both.append(total.reshape(half, TILE, 4 * channels))
            tile = jnp.concatenate(both, axis=1).astype(jnp.bfloat16)
            start = pl.multiple_of(group * (QUADS * TILE) + pair * 2 * TILE, 2 * TILE)
            cross[:, 0, pl.ds(start, 2 * TILE), :] = tile[:, :, :2 * channels]
            cross[:, 1, pl.ds(start, 2 * TILE), :] = tile[:, :, 2 * channels:]
        return carry

    lax.fori_loop(0, groups, group_step, 0, unroll=2)


def lag_chunk(ch, chunks, scaling, t_ref, cross, sums, send):
    count, quarters, channels, width = sums.shape
    size = 2 * cross.shape[2]

    def pair_step(p, carry):
        wide = jnp.concatenate([cross[2 * p].reshape(size, width // 2),
                                cross[2 * p + 1].reshape(size, width // 2)], axis=1)
        total = jnp.dot(t_ref[:, ch * size:(ch + 1) * size], wide,
                        preferred_element_type=jnp.float32)
        if ch:
            total = total + sums[p].reshape(quarters * channels, width)
        if ch == chunks - 1:
            total = (total * scaling).T
        sums[p] = total.reshape(quarters, channels, width)
        if ch == chunks - 1:
            for n in range(quarters):
                send(p, n).start()
        return carry

    lax.fori_loop(0, count, pair_step, 0, unroll=2)


def spread_kernel(reach, chans, wins, chunks, scaling, pair_ref, p_ref, t_ref, o_ref, cross, sums,
                  out_sem, own_sem, s1, r1, s2, r2, s3, r3, *bufs):
    chan = lax.axis_index("chan")
    win = lax.axis_index("win")
    row = win // CORES
    core = lax.rem(win, CORES)
    rows = wins // CORES
    other = row * CORES + (CORES - 1 - core)
    own = reach - 1
    size = p_ref.shape[0] // chunks
    offsets = list(range(1 - reach, reach + 1))
    order = sorted((o for o in offsets if o != 0), key=abs)

    def at(c):
        return lax.rem(c + chans, chans)

    def peer(step):
        return lax.rem(row + step + rows, rows) * CORES + core

    friends = sorted({o % chans for o in offsets if o} | {-o % chans for o in offsets if o})
    barrier = pltpu.get_barrier_semaphore()
    for f in friends:
        pl.semaphore_signal(barrier, inc=1, device_id=(at(chan + f), win), device_id_type=MESH)
    for step in range(1, rows):
        pl.semaphore_signal(barrier, inc=1, device_id=(chan, peer(step)), device_id_type=MESH)
    pl.semaphore_signal(barrier, inc=1, device_id=(chan, other), device_id_type=MESH)
    pl.semaphore_wait(barrier, len(friends) + rows)

    def mine(ch):
        return pltpu.make_async_copy(origin(own, 0, ch), place(own, win, ch), own_sem.at[ch])

    def place(slot, piece, ch):
        return bufs[ch].at[slot, piece]

    def origin(slot, step, ch):
        if slot == own and step == 0:
            return p_ref.at[pl.ds(ch * size, size)]
        return place(slot, peer(-step), ch)

    def whole_way(o, ch):
        return abs(o) == 1 and ch % 2 == 0

    def along(o, step, ch):
        slot = o + own
        return pltpu.make_async_remote_copy(
            src_ref=origin(own, step, ch), dst_ref=place(slot, peer(-step), ch),
            send_sem=s1.at[slot, step, ch], recv_sem=r1.at[slot, step, ch],
            device_id=(at(chan - o), win), device_id_type=MESH)

    def across(slot, step, ch):
        return pltpu.make_async_remote_copy(
            src_ref=origin(slot, 0, ch), dst_ref=place(slot, win, ch),
            send_sem=s2.at[slot, step, ch], recv_sem=r2.at[slot, step, ch],
            device_id=(chan, peer(step)), device_id_type=MESH)

    def arrived(slot, step, ch):
        here = place(slot, peer(-step), ch)
        return pltpu.make_async_remote_copy(
            src_ref=here, dst_ref=here, send_sem=s2.at[slot, step, ch],
            recv_sem=r2.at[slot, step, ch], device_id=(chan, peer(step)), device_id_type=MESH)

    def beside(slot, step, ch):
        return pltpu.make_async_remote_copy(
            src_ref=origin(slot, step, ch), dst_ref=place(slot, peer(-step), ch),
            send_sem=s3.at[slot, step, ch], recv_sem=r3.at[slot, step, ch],
            device_id=(chan, other), device_id_type=MESH)

    def from_beside(slot, step, ch):
        base = lax.rem(row - step + rows, rows) * CORES + (CORES - 1 - core)
        here = place(slot, base, ch)
        return pltpu.make_async_remote_copy(
            src_ref=here, dst_ref=here, send_sem=s3.at[slot, step, ch],
            recv_sem=r3.at[slot, step, ch], device_id=(chan, other), device_id_type=MESH)

    steps = range(1, rows)

    def begin(ch):
        for step in steps:
            across(own, step, ch).start()
        for o in order:
            along(o, 0, ch).start()
        beside(own, 0, ch).start()
        mine(ch).start()

    def send(p, n):
        return pltpu.make_async_copy(
            sums.at[p, n], o_ref.at[n % 2, 2 * p + n // 2], out_sem.at[p, n])

    def second(ch):
        for step in steps:
            arrived(own, step, ch).wait_recv()
            for o in order:
                if whole_way(o, ch):
                    along(o, step, ch).start()
            beside(own, step, ch).start()
        for o in order:
            along(o, 0, ch).wait_recv()
            if not whole_way(o, ch):
                for step in steps:
                    across(o + own, step, ch).start()
            beside(o + own, 0, ch).start()

    def third(ch):
        for o in order:
            for step in steps:
                if whole_way(o, ch):
                    along(o, step, ch).wait_recv()
                else:
                    arrived(o + own, step, ch).wait_recv()
                beside(o + own, step, ch).start()

    pick = [jnp.minimum(lax.rem(pair_ref[0, n] - (chan - own) + 2 * chans, chans), 2 * reach - 1)
            for n in range(2)]

    def compute(ch):
        mine(ch).wait()
        for o in offsets:
            for step in range(rows):
                from_beside(o + own, step, ch).wait_recv()
        cross_chunk(pick, bufs[ch], cross)
        lag_chunk(ch, chunks, scaling, t_ref, cross, sums, send)

    begin(0)
    begin(1)
    for ch in range(chunks + 2):
        if ch < chunks:
            second(ch)
        if ch + 2 < chunks:
            begin(ch + 2)
        if 0 <= ch - 1 < chunks:
            third(ch - 1)
        if ch - 2 >= 0:
            compute(ch - 2)
    for ch in range(chunks):
        for o in offsets:
            for step in range(rows):
                if o != 0 and (step == 0 or whole_way(o, ch)):
                    along(o, step, ch).wait_send()
                if step > 0 and (o == 0 or not whole_way(o, ch)):
                    across(o + own, step, ch).wait_send()
                beside(o + own, step, ch).wait_send()

    def drain(p, carry):
        for n in range(sums.shape[1]):
            send(p, n).wait()
        return carry

    lax.fori_loop(0, sums.shape[0], drain, 0)


def spread(pairs, piece, table, scaling, reach, chans, wins, chunks):
    slots = 2 * reach
    rows = wins // CORES
    groups, channels, lanes = piece.shape
    lags, bins = table.shape[0], table.shape[1] // 2
    half = channels // 2
    size = groups // chunks
    sems = pltpu.SemaphoreType.DMA((slots, rows, chunks))
    buf = pltpu.VMEM((slots, wins, size, channels, lanes), piece.dtype)
    vmem = pl.BlockSpec(memory_space=pltpu.VMEM)
    out = pl.pallas_call(
        functools.partial(spread_kernel, reach, chans, wins, chunks, scaling),
        out_shape=jax.ShapeDtypeStruct((2, half, channels, lags), jnp.float32),
        in_specs=[pl.BlockSpec(memory_space=pltpu.SMEM), vmem, vmem],
        out_specs=pl.BlockSpec(memory_space=pl.ANY),
        scratch_shapes=[pltpu.VMEM((half, 2, bins // chunks, 2 * channels), jnp.bfloat16),
                        pltpu.VMEM((half // 2, 4, channels, lags), jnp.float32),
                        pltpu.SemaphoreType.DMA((half // 2, 4)),
                        pltpu.SemaphoreType.DMA((chunks,))] + [sems] * 6 + [buf] * chunks,
        compiler_params=pltpu.CompilerParams(
            collective_id=0, has_side_effects=True, vmem_limit_bytes=56 * 2**20),
        name="spread",
    )(pairs, piece, table)
    return out.reshape(1, channels, channels, lags)


def per_device(chans, wins, spectra, pair_blocks):
    whitened = whiten(spectra)
    length_bins = spectra.shape[3]
    reach = pair_blocks.shape[0] * wins // 2
    chunks = 8 if wins <= 2 * CORES else 4
    table = make_table(length_bins).reshape(NLAG, 2, chunks, -1).transpose(0, 2, 1, 3)
    table = jnp.asarray(table.reshape(NLAG, 2 * length_bins))
    scaling = 1.0 / math.sqrt(spectra.shape[1] * wins * length_bins)
    return spread(pair_blocks, arrange(whitened), table, scaling, reach, chans, wins, chunks)


def solution(mesh):
    in_specs = (P(None, "win", "chan", None), P(("chan", "win"), None))
    out_specs = P(("chan", "win"), None, None, None)
    return jax.shard_map(
        functools.partial(per_device, mesh.shape["chan"], mesh.shape["win"]),
        mesh=mesh, in_specs=in_specs, out_specs=out_specs, check_vma=False
    )
```

```python
import functools
import math

import jax
import jax.numpy as jnp
import ml_dtypes
import numpy as np
from jax import lax
from jax.experimental import pallas as pl
from jax.experimental.pallas import tpu as pltpu
from jax.sharding import PartitionSpec as P

NLAG = 256
HALF_BAND = 64
MESH = pl.DeviceIdType.MESH

eps = 1e-05
first_bin = 60.0
samples = 15000.0

CORES = 2
TILE = 8
QUADS = 4


def smoothing(length_bins, half_width):
    indices = jnp.arange(length_bins, dtype=jnp.int32)
    return (jnp.abs(indices[:, None] - indices[None, :]) <= half_width).astype(jnp.float32)


def whiten(spectra):
    length_bins = spectra.shape[-1]
    real_part = spectra[0].astype(jnp.float32)
    imag_part = spectra[1].astype(jnp.float32)
    powers = real_part * real_part + imag_part * imag_part
    smoother = smoothing(length_bins, HALF_BAND)
    counts = jnp.sum(smoother, axis=0)
    rows_flat = powers.reshape(-1, length_bins)
    smooth = jnp.dot(rows_flat, smoother, precision=lax.Precision.HIGHEST) / counts
    factor = lax.rsqrt(smooth + eps).reshape(powers.shape)
    return jnp.stack([real_part * factor, imag_part * factor]).astype(jnp.bfloat16)


def make_table(length_bins):
    bin_freq = np.float32(first_bin) + np.arange(length_bins, dtype=np.float32)
    lag_steps = np.arange(NLAG, dtype=np.float32) - np.float32(NLAG // 2)
    angles = np.float32(2.0 * math.pi / samples) * bin_freq[None, :] * lag_steps[:, None]
    return np.concatenate([np.cos(angles), -np.sin(angles)], axis=1).astype(ml_dtypes.bfloat16)


def arrange_kernel(x_ref, o_ref, turned):
    parts, channels, bins = x_ref.shape
    groups = bins // (QUADS * TILE)
    me = lax.rem(lax.axis_index("win"), QUADS)
    for part in range(parts):
        flipped = x_ref[part].astype(jnp.float32).T
        turned[part] = flipped.reshape(groups, QUADS, TILE, channels)

    def group_step(group, carry):
        rows = []
        for part in range(parts):
            for place in range(QUADS):
                quad = lax.rem(place - me + QUADS, QUADS)
                rows.append(turned[part, group, quad])
        o_ref[group] = jnp.concatenate(rows, axis=0).T.astype(o_ref.dtype)
        return carry

    lax.fori_loop(0, groups, group_step, 0, unroll=4)


def arrange(whitened):
    parts = whitened.shape[0] * whitened.shape[1]
    channels, bins = whitened.shape[2:]
    groups = bins // (QUADS * TILE)
    lanes = parts * QUADS * TILE
    return pl.pallas_call(
        arrange_kernel,
        out_shape=jax.ShapeDtypeStruct((groups, channels, lanes), jnp.bfloat16),
        in_specs=[pl.BlockSpec(memory_space=pltpu.VMEM)],
        out_specs=pl.BlockSpec(memory_space=pltpu.VMEM),
        scratch_shapes=[pltpu.VMEM((parts, groups, QUADS, TILE, channels), jnp.float32)],
        compiler_params=pltpu.CompilerParams(vmem_limit_bytes=24 * 2**20),
        name="arrange",
    )(whitened.reshape(parts, channels, bins))


def cross_chunk(pick, buf, cross):
    _, wins, groups, channels, lanes = buf.shape
    half = channels // 2
    lane = lax.broadcasted_iota(jnp.int32, (1, lanes), 1)
    place = (lane // TILE) % QUADS
    keep = lax.broadcasted_iota(jnp.int32, (2 * TILE, lanes), 0) % TILE == lax.broadcasted_iota(
        jnp.int32, (2 * TILE, lanes), 1) % TILE
    keep = keep.astype(jnp.float32).astype(jnp.bfloat16)[None]
    sign = jnp.where(lane < lanes // 2, -1.0, 1.0)
    zero = jnp.zeros((channels, lanes), jnp.bfloat16)

    def merged(pieces, quad):
        out = pieces[0]
        for m in range(1, QUADS):
            out = jnp.where(place == (m + quad) % QUADS, pieces[m], out)
        return out

    def spread_rows(x):
        wide = jnp.broadcast_to(x[:, None, :], (half, TILE, lanes))
        wide = wide.reshape(half * TILE // (2 * TILE), 2 * TILE, lanes).astype(jnp.bfloat16) * keep
        return wide.reshape(half * TILE, lanes)

    def group_step(group, carry):
        a_pieces = [buf[pick[0], m, group].astype(jnp.float32) for m in range(wins)]
        b_pieces = [buf[pick[1], m, group].astype(jnp.float32) for m in range(wins)]
        for pair in range(QUADS // 2):
            both = []
            for quad in (2 * pair, 2 * pair + 1):
                total = None
                for bundle in range(0, wins, QUADS):
                    a = merged(a_pieces[bundle:bundle + QUADS], quad)
                    b = merged(b_pieces[bundle:bundle + QUADS], quad)
                    bx = (pltpu.roll(b, lanes // 2, 1) * sign).astype(jnp.bfloat16)
                    b = b.astype(jnp.bfloat16)
                    left = jnp.concatenate([spread_rows(a[:half]), spread_rows(a[half:])], axis=1)
                    right = jnp.concatenate(
                        [jnp.concatenate([b, zero, bx, zero], axis=0),
                         jnp.concatenate([zero, b, zero, bx], axis=0)], axis=1)
                    prod = lax.dot_general(left, right, (((1,), (1,)), ((), ())),
                                           preferred_element_type=jnp.float32)
                    total = prod if total is None else total + prod
                both.append(total.reshape(half, TILE, 4 * channels))
            tile = jnp.concatenate(both, axis=1).astype(jnp.bfloat16)
            start = pl.multiple_of(group * (QUADS * TILE) + pair * 2 * TILE, 2 * TILE)
            cross[:, 0, pl.ds(start, 2 * TILE), :] = tile[:, :, :2 * channels]
            cross[:, 1, pl.ds(start, 2 * TILE), :] = tile[:, :, 2 * channels:]
        return carry

    lax.fori_loop(0, groups, group_step, 0, unroll=2)


def lag_chunk(ch, chunks, t_ref, cross, sums, send):
    count, quarters, channels, width = sums.shape
    size = 2 * cross.shape[2]

    def pair_step(p, carry):
        wide = jnp.concatenate([cross[2 * p].reshape(size, width // 2),
                                cross[2 * p + 1].reshape(size, width // 2)], axis=1)
        total = jnp.dot(t_ref[:, ch * size:(ch + 1) * size], wide,
                        preferred_element_type=jnp.float32)
        if ch:
            total = total + sums[p].reshape(quarters * channels, width)
        if ch == chunks - 1:
            total = total.T
        sums[p] = total.reshape(quarters, channels, width)
        if ch == chunks - 1:
            for n in range(quarters):
                send(p, n).start()
        return carry

    lax.fori_loop(0, count, pair_step, 0, unroll=2)


def spread_kernel(reach, chans, wins, chunks, pair_ref, p_ref, t_ref, o_ref, cross, sums,
                  out_sem, own_sem, s1, r1, s2, r2, s3, r3, *bufs):
    chan = lax.axis_index("chan")
    win = lax.axis_index("win")
    row = win // CORES
    core = lax.rem(win, CORES)
    rows = wins // CORES
    other = row * CORES + (CORES - 1 - core)
    own = reach - 1
    size = p_ref.shape[0] // chunks
    offsets = list(range(1 - reach, reach + 1))
    order = sorted((o for o in offsets if o != 0), key=abs)

    def at(c):
        return lax.rem(c + chans, chans)

    def peer(step):
        return lax.rem(row + step + rows, rows) * CORES + core

    friends = sorted({o % chans for o in offsets if o} | {-o % chans for o in offsets if o})
    barrier = pltpu.get_barrier_semaphore()
    for f in friends:
        pl.semaphore_signal(barrier, inc=1, device_id=(at(chan + f), win), device_id_type=MESH)
    for step in range(1, rows):
        pl.semaphore_signal(barrier, inc=1, device_id=(chan, peer(step)), device_id_type=MESH)
    pl.semaphore_signal(barrier, inc=1, device_id=(chan, other), device_id_type=MESH)
    pl.semaphore_wait(barrier, len(friends) + rows)

    def mine(ch):
        return pltpu.make_async_copy(origin(own, 0, ch), place(own, win, ch), own_sem.at[ch])

    def place(slot, piece, ch):
        return bufs[ch].at[slot, piece]

    def origin(slot, step, ch):
        if slot == own and step == 0:
            return p_ref.at[pl.ds(ch * size, size)]
        return place(slot, peer(-step), ch)

    def whole_way(o, ch):
        return abs(o) == 1 and ch % 2 == 0

    def along(o, step, ch):
        slot = o + own
        return pltpu.make_async_remote_copy(
            src_ref=origin(own, step, ch), dst_ref=place(slot, peer(-step), ch),
            send_sem=s1.at[slot, step, ch], recv_sem=r1.at[slot, step, ch],
            device_id=(at(chan - o), win), device_id_type=MESH)

    def across(slot, step, ch):
        return pltpu.make_async_remote_copy(
            src_ref=origin(slot, 0, ch), dst_ref=place(slot, win, ch),
            send_sem=s2.at[slot, step, ch], recv_sem=r2.at[slot, step, ch],
            device_id=(chan, peer(step)), device_id_type=MESH)

    def arrived(slot, step, ch):
        here = place(slot, peer(-step), ch)
        return pltpu.make_async_remote_copy(
            src_ref=here, dst_ref=here, send_sem=s2.at[slot, step, ch],
            recv_sem=r2.at[slot, step, ch], device_id=(chan, peer(step)), device_id_type=MESH)

    def beside(slot, step, ch):
        return pltpu.make_async_remote_copy(
            src_ref=origin(slot, step, ch), dst_ref=place(slot, peer(-step), ch),
            send_sem=s3.at[slot, step, ch], recv_sem=r3.at[slot, step, ch],
            device_id=(chan, other), device_id_type=MESH)

    def from_beside(slot, step, ch):
        base = lax.rem(row - step + rows, rows) * CORES + (CORES - 1 - core)
        here = place(slot, base, ch)
        return pltpu.make_async_remote_copy(
            src_ref=here, dst_ref=here, send_sem=s3.at[slot, step, ch],
            recv_sem=r3.at[slot, step, ch], device_id=(chan, other), device_id_type=MESH)

    steps = range(1, rows)

    def begin(ch):
        for step in steps:
            across(own, step, ch).start()
        for o in order:
            along(o, 0, ch).start()
        beside(own, 0, ch).start()
        mine(ch).start()

    def send(p, n):
        return pltpu.make_async_copy(
            sums.at[p, n], o_ref.at[n % 2, 2 * p + n // 2], out_sem.at[p, n])

    def second(ch):
        for step in steps:
            arrived(own, step, ch).wait_recv()
            for o in order:
                if whole_way(o, ch):
                    along(o, step, ch).start()
            beside(own, step, ch).start()
        for o in order:
            along(o, 0, ch).wait_recv()
            if not whole_way(o, ch):
                for step in steps:
                    across(o + own, step, ch).start()
            beside(o + own, 0, ch).start()

    def third(ch):
        for o in order:
            for step in steps:
                if whole_way(o, ch):
                    along(o, step, ch).wait_recv()
                else:
                    arrived(o + own, step, ch).wait_recv()
                beside(o + own, step, ch).start()

    pick = [jnp.minimum(lax.rem(pair_ref[0, n] - (chan - own) + 2 * chans, chans), 2 * reach - 1)
            for n in range(2)]

    def compute(ch):
        mine(ch).wait()
        for o in offsets:
            for step in range(rows):
                from_beside(o + own, step, ch).wait_recv()
        cross_chunk(pick, bufs[ch], cross)
        lag_chunk(ch, chunks, t_ref, cross, sums, send)

    ahead = 3
    for ch in range(ahead):
        begin(ch)
    for ch in range(chunks + ahead):
        if ch < chunks:
            second(ch)
        if ch + ahead < chunks:
            begin(ch + ahead)
        if ch == chunks + 1:
            compute(ch - ahead)
        if 0 <= ch - 2 < chunks:
            third(ch - 2)
        if ch >= ahead and ch != chunks + 1:
            compute(ch - ahead)
    for ch in range(chunks):
        for o in offsets:
            for step in range(rows):
                if o != 0 and (step == 0 or whole_way(o, ch)):
                    along(o, step, ch).wait_send()
                if step > 0 and (o == 0 or not whole_way(o, ch)):
                    across(o + own, step, ch).wait_send()
                beside(o + own, step, ch).wait_send()

    def drain(p, carry):
        for n in range(sums.shape[1]):
            send(p, n).wait()
        return carry

    lax.fori_loop(0, sums.shape[0], drain, 0)


def spread(pairs, piece, table, scaling, reach, chans, wins, chunks):
    slots = 2 * reach
    rows = wins // CORES
    groups, channels, lanes = piece.shape
    lags, bins = table.shape[0], table.shape[1] // 2
    half = channels // 2
    size = groups // chunks
    sems = pltpu.SemaphoreType.DMA((slots, rows, chunks))
    buf = pltpu.VMEM((slots, wins, size, channels, lanes), piece.dtype)
    vmem = pl.BlockSpec(memory_space=pltpu.VMEM)
    out = pl.pallas_call(
        functools.partial(spread_kernel, reach, chans, wins, chunks),
        out_shape=jax.ShapeDtypeStruct((2, half, channels, lags), jnp.float32),
        in_specs=[pl.BlockSpec(memory_space=pltpu.SMEM), vmem, vmem],
        out_specs=pl.BlockSpec(memory_space=pl.ANY),
        scratch_shapes=[pltpu.VMEM((half, 2, bins // chunks, 2 * channels), jnp.bfloat16),
                        pltpu.VMEM((half // 2, 4, channels, lags), jnp.float32),
                        pltpu.SemaphoreType.DMA((half // 2, 4)),
                        pltpu.SemaphoreType.DMA((chunks,))] + [sems] * 6 + [buf] * chunks,
        compiler_params=pltpu.CompilerParams(
            collective_id=0, has_side_effects=True, vmem_limit_bytes=56 * 2**20),
        name="spread",
    )(pairs, piece, table)
    return out.reshape(1, channels, channels, lags) * scaling


def per_device(chans, wins, spectra, pair_blocks):
    whitened = whiten(spectra)
    length_bins = spectra.shape[3]
    reach = pair_blocks.shape[0] * wins // 2
    chunks = 8 if wins <= 2 * CORES else 4
    table = make_table(length_bins).reshape(NLAG, 2, chunks, -1).transpose(0, 2, 1, 3)
    table = jnp.asarray(table.reshape(NLAG, 2 * length_bins))
    scaling = 1.0 / math.sqrt(spectra.shape[1] * wins * length_bins)
    return spread(pair_blocks, arrange(whitened), table, scaling, reach, chans, wins, chunks)


def solution(mesh):
    in_specs = (P(None, "win", "chan", None), P(("chan", "win"), None))
    out_specs = P(("chan", "win"), None, None, None)
    return jax.shard_map(
        functools.partial(per_device, mesh.shape["chan"], mesh.shape["win"]),
        mesh=mesh, in_specs=in_specs, out_specs=out_specs, check_vma=False
    )
```

```python
import functools
import math

import jax
import jax.numpy as jnp
import ml_dtypes
import numpy as np
from jax import lax
from jax.experimental import pallas as pl
from jax.experimental.pallas import tpu as pltpu
from jax.sharding import PartitionSpec as P

NLAG = 256
HALF_BAND = 64
MESH = pl.DeviceIdType.MESH

eps = 1e-05
first_bin = 60.0
samples = 15000.0

CORES = 2
TILE = 8
QUADS = 4


def smoothing(length_bins, half_width):
    indices = jnp.arange(length_bins, dtype=jnp.int32)
    return (jnp.abs(indices[:, None] - indices[None, :]) <= half_width).astype(jnp.float32)


def whiten(spectra):
    length_bins = spectra.shape[-1]
    real_part = spectra[0].astype(jnp.float32)
    imag_part = spectra[1].astype(jnp.float32)
    powers = real_part * real_part + imag_part * imag_part
    smoother = smoothing(length_bins, HALF_BAND)
    counts = jnp.sum(smoother, axis=0)
    rows_flat = powers.reshape(-1, length_bins)
    smooth = jnp.dot(rows_flat, smoother, precision=lax.Precision.HIGHEST) / counts
    factor = lax.rsqrt(smooth + eps).reshape(powers.shape)
    return jnp.stack([real_part * factor, imag_part * factor]).astype(jnp.bfloat16)


def make_table(length_bins):
    bin_freq = np.float32(first_bin) + np.arange(length_bins, dtype=np.float32)
    lag_steps = np.arange(NLAG, dtype=np.float32) - np.float32(NLAG // 2)
    angles = np.float32(2.0 * math.pi / samples) * bin_freq[None, :] * lag_steps[:, None]
    return np.concatenate([np.cos(angles), -np.sin(angles)], axis=1).astype(ml_dtypes.bfloat16)


def arrange_kernel(x_ref, o_ref, turned):
    parts, channels, bins = x_ref.shape
    groups = bins // (QUADS * TILE)
    me = lax.rem(lax.axis_index("win"), QUADS)
    for part in range(parts):
        flipped = x_ref[part].astype(jnp.float32).T
        turned[part] = flipped.reshape(groups, QUADS, TILE, channels)

    def group_step(group, carry):
        rows = []
        for part in range(parts):
            for place in range(QUADS):
                quad = lax.rem(place - me + QUADS, QUADS)
                rows.append(turned[part, group, quad])
        o_ref[group] = jnp.concatenate(rows, axis=0).T.astype(o_ref.dtype)
        return carry

    lax.fori_loop(0, groups, group_step, 0, unroll=4)


def arrange(whitened):
    parts = whitened.shape[0] * whitened.shape[1]
    channels, bins = whitened.shape[2:]
    groups = bins // (QUADS * TILE)
    lanes = parts * QUADS * TILE
    return pl.pallas_call(
        arrange_kernel,
        out_shape=jax.ShapeDtypeStruct((groups, channels, lanes), jnp.bfloat16),
        in_specs=[pl.BlockSpec(memory_space=pltpu.VMEM)],
        out_specs=pl.BlockSpec(memory_space=pltpu.VMEM),
        scratch_shapes=[pltpu.VMEM((parts, groups, QUADS, TILE, channels), jnp.float32)],
        compiler_params=pltpu.CompilerParams(vmem_limit_bytes=24 * 2**20),
        name="arrange",
    )(whitened.reshape(parts, channels, bins))


def cross_chunk(pick, buf, cross):
    _, wins, groups, channels, lanes = buf.shape
    half = channels // 2
    lane = lax.broadcasted_iota(jnp.int32, (1, lanes), 1)
    place = (lax.broadcasted_iota(jnp.int32, (channels, lanes), 1) // TILE) % QUADS
    keep = lax.broadcasted_iota(jnp.int32, (2 * TILE, lanes), 0) % TILE == lax.broadcasted_iota(
        jnp.int32, (2 * TILE, lanes), 1) % TILE
    keep = keep.astype(jnp.float32).astype(jnp.bfloat16)[None]
    sign = jnp.where(lane < lanes // 2, -1.0, 1.0)
    zero = jnp.zeros((channels, lanes), jnp.bfloat16)

    def merged(pieces, quad):
        out = pieces[0]
        for m in range(1, QUADS):
            out = jnp.where(place == (m + quad) % QUADS, pieces[m], out)
        return out


    def spread_rows(x):
        wide = jnp.broadcast_to(x[:, None, :], (half, TILE, lanes))
        wide = wide.reshape(half * TILE // (2 * TILE), 2 * TILE, lanes).astype(jnp.bfloat16) * keep
        return wide.reshape(half * TILE, lanes)

    def group_step(group, carry):
        a_pieces = [buf[pick[0], m, group] for m in range(wins)]
        b_pieces = [buf[pick[1], m, group] for m in range(wins)]
        for pair in range(QUADS // 2):
            both = []
            for quad in (2 * pair, 2 * pair + 1):
                total = None
                for bundle in range(0, wins, QUADS):
                    a = merged(a_pieces[bundle:bundle + QUADS], quad).astype(jnp.float32)
                    b = merged(b_pieces[bundle:bundle + QUADS], quad)
                    bx = (pltpu.roll(b.astype(jnp.float32), lanes // 2, 1) * sign).astype(jnp.bfloat16)
                    left = jnp.concatenate([spread_rows(a[:half]), spread_rows(a[half:])], axis=1)
                    right = jnp.concatenate(
                        [jnp.concatenate([b, zero, bx, zero], axis=0),
                         jnp.concatenate([zero, b, zero, bx], axis=0)], axis=1)
                    prod = lax.dot_general(left, right, (((1,), (1,)), ((), ())),
                                           preferred_element_type=jnp.float32)
                    total = prod if total is None else total + prod
                both.append(total.reshape(half, TILE, 4 * channels))
            tile = jnp.concatenate(both, axis=1).astype(jnp.bfloat16)
            start = pl.multiple_of(group * (QUADS * TILE) + pair * 2 * TILE, 2 * TILE)
            cross[:, 0, pl.ds(start, 2 * TILE), :] = tile[:, :, :2 * channels]
            cross[:, 1, pl.ds(start, 2 * TILE), :] = tile[:, :, 2 * channels:]
        return carry

    lax.fori_loop(0, groups, group_step, 0, unroll=2)


def lag_chunk(ch, chunks, t_ref, cross, sums, send):
    count, quarters, channels, width = sums.shape
    size = 2 * cross.shape[2]

    def pair_step(p, carry):
        wide = jnp.concatenate([cross[2 * p].reshape(size, width // 2),
                                cross[2 * p + 1].reshape(size, width // 2)], axis=1)
        total = jnp.dot(t_ref[:, ch * size:(ch + 1) * size], wide,
                        preferred_element_type=jnp.float32)
        if ch:
            total = total + sums[p].reshape(quarters * channels, width)
        if ch == chunks - 1:
            total = total.T
        sums[p] = total.reshape(quarters, channels, width)
        if ch == chunks - 1:
            for n in range(quarters):
                send(p, n).start()
        return carry

    lax.fori_loop(0, count, pair_step, 0, unroll=2)


def spread_kernel(reach, chans, wins, chunks, pair_ref, p_ref, t_ref, o_ref, cross, sums,
                  out_sem, own_sem, s1, r1, s2, r2, s3, r3, *bufs):
    chan = lax.axis_index("chan")
    win = lax.axis_index("win")
    row = win // CORES
    core = lax.rem(win, CORES)
    rows = wins // CORES
    other = row * CORES + (CORES - 1 - core)
    own = reach - 1
    size = p_ref.shape[0] // chunks
    offsets = list(range(1 - reach, reach + 1))
    order = sorted((o for o in offsets if o != 0), key=abs)

    def at(c):
        return lax.rem(c + chans, chans)

    def peer(step):
        return lax.rem(row + step + rows, rows) * CORES + core

    friends = sorted({o % chans for o in offsets if o} | {-o % chans for o in offsets if o})
    barrier = pltpu.get_barrier_semaphore()
    for f in friends:
        pl.semaphore_signal(barrier, inc=1, device_id=(at(chan + f), win), device_id_type=MESH)
    for step in range(1, rows):
        pl.semaphore_signal(barrier, inc=1, device_id=(chan, peer(step)), device_id_type=MESH)
    pl.semaphore_signal(barrier, inc=1, device_id=(chan, other), device_id_type=MESH)
    pl.semaphore_wait(barrier, len(friends) + rows)

    def mine(ch):
        return pltpu.make_async_copy(origin(own, 0, ch), place(own, win, ch), own_sem.at[ch])

    def place(slot, piece, ch):
        return bufs[ch].at[slot, piece]

    def origin(slot, step, ch):
        if slot == own and step == 0:
            return p_ref.at[pl.ds(ch * size, size)]
        return place(slot, peer(-step), ch)

    def whole_way(o, ch):
        return abs(o) == 1 and ch % 2 == 0

    def along(o, step, ch):
        slot = o + own
        return pltpu.make_async_remote_copy(
            src_ref=origin(own, step, ch), dst_ref=place(slot, peer(-step), ch),
            send_sem=s1.at[slot, step, ch], recv_sem=r1.at[slot, step, ch],
            device_id=(at(chan - o), win), device_id_type=MESH)

    def across(slot, step, ch):
        return pltpu.make_async_remote_copy(
            src_ref=origin(slot, 0, ch), dst_ref=place(slot, win, ch),
            send_sem=s2.at[slot, step, ch], recv_sem=r2.at[slot, step, ch],
            device_id=(chan, peer(step)), device_id_type=MESH)

    def arrived(slot, step, ch):
        here = place(slot, peer(-step), ch)
        return pltpu.make_async_remote_copy(
            src_ref=here, dst_ref=here, send_sem=s2.at[slot, step, ch],
            recv_sem=r2.at[slot, step, ch], device_id=(chan, peer(step)), device_id_type=MESH)

    def beside(slot, step, ch):
        return pltpu.make_async_remote_copy(
            src_ref=origin(slot, step, ch), dst_ref=place(slot, peer(-step), ch),
            send_sem=s3.at[slot, step, ch], recv_sem=r3.at[slot, step, ch],
            device_id=(chan, other), device_id_type=MESH)

    def from_beside(slot, step, ch):
        base = lax.rem(row - step + rows, rows) * CORES + (CORES - 1 - core)
        here = place(slot, base, ch)
        return pltpu.make_async_remote_copy(
            src_ref=here, dst_ref=here, send_sem=s3.at[slot, step, ch],
            recv_sem=r3.at[slot, step, ch], device_id=(chan, other), device_id_type=MESH)

    steps = range(1, rows)

    def begin(ch):
        for step in steps:
            across(own, step, ch).start()
        for o in order:
            along(o, 0, ch).start()
        beside(own, 0, ch).start()
        mine(ch).start()

    def send(p, n):
        return pltpu.make_async_copy(
            sums.at[p, n], o_ref.at[n % 2, 2 * p + n // 2], out_sem.at[p, n])

    def second(ch):
        for step in steps:
            arrived(own, step, ch).wait_recv()
            for o in order:
                if whole_way(o, ch):
                    along(o, step, ch).start()
            beside(own, step, ch).start()
        for o in order:
            along(o, 0, ch).wait_recv()
            if not whole_way(o, ch):
                for step in steps:
                    across(o + own, step, ch).start()
            beside(o + own, 0, ch).start()

    def third(ch):
        for o in order:
            for step in steps:
                if whole_way(o, ch):
                    along(o, step, ch).wait_recv()
                else:
                    arrived(o + own, step, ch).wait_recv()
                beside(o + own, step, ch).start()

    pick = [jnp.minimum(lax.rem(pair_ref[0, n] - (chan - own) + 2 * chans, chans), 2 * reach - 1)
            for n in range(2)]

    def compute(ch):
        mine(ch).wait()
        for o in offsets:
            for step in range(rows):
                from_beside(o + own, step, ch).wait_recv()
        cross_chunk(pick, bufs[ch], cross)
        lag_chunk(ch, chunks, t_ref, cross, sums, send)

    begin(0)
    begin(1)
    for ch in range(chunks + 2):
        if ch < chunks:
            second(ch)
        if ch + 2 < chunks:
            begin(ch + 2)
        if 0 <= ch - 1 < chunks:
            third(ch - 1)
        if ch - 2 >= 0:
            compute(ch - 2)
    for ch in range(chunks):
        for o in offsets:
            for step in range(rows):
                if o != 0 and (step == 0 or whole_way(o, ch)):
                    along(o, step, ch).wait_send()
                if step > 0 and (o == 0 or not whole_way(o, ch)):
                    across(o + own, step, ch).wait_send()
                beside(o + own, step, ch).wait_send()

    def drain(p, carry):
        for n in range(sums.shape[1]):
            send(p, n).wait()
        return carry

    lax.fori_loop(0, sums.shape[0], drain, 0)


def spread(pairs, piece, table, scaling, reach, chans, wins, chunks):
    slots = 2 * reach
    rows = wins // CORES
    groups, channels, lanes = piece.shape
    lags, bins = table.shape[0], table.shape[1] // 2
    half = channels // 2
    size = groups // chunks
    sems = pltpu.SemaphoreType.DMA((slots, rows, chunks))
    buf = pltpu.VMEM((slots, wins, size, channels, lanes), piece.dtype)
    vmem = pl.BlockSpec(memory_space=pltpu.VMEM)
    out = pl.pallas_call(
        functools.partial(spread_kernel, reach, chans, wins, chunks),
        out_shape=jax.ShapeDtypeStruct((2, half, channels, lags), jnp.float32),
        in_specs=[pl.BlockSpec(memory_space=pltpu.SMEM), vmem, vmem],
        out_specs=pl.BlockSpec(memory_space=pl.ANY),
        scratch_shapes=[pltpu.VMEM((half, 2, bins // chunks, 2 * channels), jnp.bfloat16),
                        pltpu.VMEM((half // 2, 4, channels, lags), jnp.float32),
                        pltpu.SemaphoreType.DMA((half // 2, 4)),
                        pltpu.SemaphoreType.DMA((chunks,))] + [sems] * 6 + [buf] * chunks,
        compiler_params=pltpu.CompilerParams(
            collective_id=0, has_side_effects=True, vmem_limit_bytes=56 * 2**20),
        name="spread",
    )(pairs, piece, table)
    return scale(out, scaling).reshape(1, channels, channels, lags)


def scale_kernel(scaling, x_ref, o_ref):
    o_ref[...] = x_ref[...] * scaling


def scale(x, scaling):
    block = pl.BlockSpec((1, x.shape[1] // 4) + x.shape[2:], lambda h, s: (h, s, 0, 0))
    return pl.pallas_call(
        functools.partial(scale_kernel, scaling),
        out_shape=jax.ShapeDtypeStruct(x.shape, x.dtype),
        grid=(x.shape[0], 4),
        in_specs=[block],
        out_specs=block,
        compiler_params=pltpu.CompilerParams(vmem_limit_bytes=60 * 2**20),
        name="scale",
    )(x)


def per_device(chans, wins, spectra, pair_blocks):
    whitened = whiten(spectra)
    length_bins = spectra.shape[3]
    reach = pair_blocks.shape[0] * wins // 2
    chunks = 8 if wins <= 2 * CORES else 4
    table = make_table(length_bins).reshape(NLAG, 2, chunks, -1).transpose(0, 2, 1, 3)
    table = jnp.asarray(table.reshape(NLAG, 2 * length_bins))
    scaling = 1.0 / math.sqrt(spectra.shape[1] * wins * length_bins)
    return spread(pair_blocks, arrange(whitened), table, scaling, reach, chans, wins, chunks)


def solution(mesh):
    in_specs = (P(None, "win", "chan", None), P(("chan", "win"), None))
    out_specs = P(("chan", "win"), None, None, None)
    return jax.shard_map(
        functools.partial(per_device, mesh.shape["chan"], mesh.shape["win"]),
        mesh=mesh, in_specs=in_specs, out_specs=out_specs, check_vma=False
    )
```

```python
import functools
import math

import jax
import jax.numpy as jnp
import ml_dtypes
import numpy as np
from jax import lax
from jax.experimental import pallas as pl
from jax.experimental.pallas import tpu as pltpu
from jax.sharding import PartitionSpec as P

NLAG = 256
HALF_BAND = 64
MESH = pl.DeviceIdType.MESH

eps = 1e-05
first_bin = 60.0
samples = 15000.0

CORES = 2
TILE = 8
QUADS = 4


def smoothing(length_bins, half_width):
    indices = jnp.arange(length_bins, dtype=jnp.int32)
    return (jnp.abs(indices[:, None] - indices[None, :]) <= half_width).astype(jnp.float32)


def whiten(spectra):
    length_bins = spectra.shape[-1]
    real_part = spectra[0].astype(jnp.float32)
    imag_part = spectra[1].astype(jnp.float32)
    powers = real_part * real_part + imag_part * imag_part
    smoother = smoothing(length_bins, HALF_BAND)
    counts = jnp.sum(smoother, axis=0)
    rows_flat = powers.reshape(-1, length_bins)
    smooth = jnp.dot(rows_flat, smoother, precision=lax.Precision.HIGHEST) / counts
    factor = lax.rsqrt(smooth + eps).reshape(powers.shape)
    return jnp.stack([real_part * factor, imag_part * factor]).astype(jnp.bfloat16)


def make_table(length_bins):
    bin_freq = np.float32(first_bin) + np.arange(length_bins, dtype=np.float32)
    lag_steps = np.arange(NLAG, dtype=np.float32) - np.float32(NLAG // 2)
    angles = np.float32(2.0 * math.pi / samples) * bin_freq[None, :] * lag_steps[:, None]
    return np.concatenate([np.cos(angles), -np.sin(angles)], axis=1).astype(ml_dtypes.bfloat16)


def arrange_kernel(x_ref, o_ref, turned):
    parts, channels, bins = x_ref.shape
    groups = bins // (QUADS * TILE)
    me = lax.rem(lax.axis_index("win"), QUADS)
    for part in range(parts):
        flipped = x_ref[part].astype(jnp.float32).T
        turned[part] = flipped.reshape(groups, QUADS, TILE, channels)

    def group_step(group, carry):
        rows = []
        for part in range(parts):
            for place in range(QUADS):
                quad = lax.rem(place - me + QUADS, QUADS)
                rows.append(turned[part, group, quad])
        o_ref[group] = jnp.concatenate(rows, axis=0).T.astype(o_ref.dtype)
        return carry

    lax.fori_loop(0, groups, group_step, 0, unroll=4)


def arrange(whitened):
    parts = whitened.shape[0] * whitened.shape[1]
    channels, bins = whitened.shape[2:]
    groups = bins // (QUADS * TILE)
    lanes = parts * QUADS * TILE
    return pl.pallas_call(
        arrange_kernel,
        out_shape=jax.ShapeDtypeStruct((groups, channels, lanes), jnp.bfloat16),
        in_specs=[pl.BlockSpec(memory_space=pltpu.VMEM)],
        out_specs=pl.BlockSpec(memory_space=pltpu.VMEM),
        scratch_shapes=[pltpu.VMEM((parts, groups, QUADS, TILE, channels), jnp.float32)],
        compiler_params=pltpu.CompilerParams(vmem_limit_bytes=24 * 2**20),
        name="arrange",
    )(whitened.reshape(parts, channels, bins))


def cross_chunk(pick, buf, cross):
    _, wins, groups, channels, lanes = buf.shape
    half = channels // 2
    lane = lax.broadcasted_iota(jnp.int32, (1, lanes), 1)
    place = (lane // TILE) % QUADS
    keep = lax.broadcasted_iota(jnp.int32, (2 * TILE, lanes), 0) % TILE == lax.broadcasted_iota(
        jnp.int32, (2 * TILE, lanes), 1) % TILE
    keep = keep.astype(jnp.float32).astype(jnp.bfloat16)[None]
    sign = jnp.where(lane < lanes // 2, -1.0, 1.0)
    zero = jnp.zeros((channels, lanes), jnp.bfloat16)

    def merged(pieces, quad):
        out = pieces[0]
        for m in range(1, QUADS):
            out = jnp.where(place == (m + quad) % QUADS, pieces[m], out)
        return out

    def spread_rows(x):
        wide = jnp.broadcast_to(x[:, None, :], (half, TILE, lanes))
        wide = wide.reshape(half * TILE // (2 * TILE), 2 * TILE, lanes).astype(jnp.bfloat16) * keep
        return wide.reshape(half * TILE, lanes)

    def group_step(group, carry):
        a_pieces = [buf[pick[0], m, group].astype(jnp.float32) for m in range(wins)]
        b_pieces = [buf[pick[1], m, group].astype(jnp.float32) for m in range(wins)]
        for pair in range(QUADS // 2):
            both = []
            for quad in (2 * pair, 2 * pair + 1):
                total = None
                for bundle in range(0, wins, QUADS):
                    a = merged(a_pieces[bundle:bundle + QUADS], quad)
                    b = merged(b_pieces[bundle:bundle + QUADS], quad)
                    bx = (pltpu.roll(b, lanes // 2, 1) * sign).astype(jnp.bfloat16)
                    b = b.astype(jnp.bfloat16)
                    left = jnp.concatenate([spread_rows(a[:half]), spread_rows(a[half:])], axis=1)
                    right = jnp.concatenate(
                        [jnp.concatenate([b, zero, bx, zero], axis=0),
                         jnp.concatenate([zero, b, zero, bx], axis=0)], axis=1)
                    prod = lax.dot_general(left, right, (((1,), (1,)), ((), ())),
                                           preferred_element_type=jnp.float32)
                    total = prod if total is None else total + prod
                both.append(total.reshape(half, TILE, 4 * channels))
            tile = jnp.concatenate(both, axis=1).astype(jnp.bfloat16)
            start = pl.multiple_of(group * (QUADS * TILE) + pair * 2 * TILE, 2 * TILE)
            cross[:, 0, pl.ds(start, 2 * TILE), :] = tile[:, :, :2 * channels]
            cross[:, 1, pl.ds(start, 2 * TILE), :] = tile[:, :, 2 * channels:]
        return carry

    lax.fori_loop(0, groups, group_step, 0, unroll=2)


def lag_chunk(ch, chunks, scaling, t_ref, cross, sums, send):
    count, quarters, channels, width = sums.shape
    size = 2 * cross.shape[2]

    def pair_step(p, carry):
        wide = jnp.concatenate([cross[2 * p].reshape(size, width // 2),
                                cross[2 * p + 1].reshape(size, width // 2)], axis=1)
        total = jnp.dot(t_ref[:, ch * size:(ch + 1) * size], wide,
                        preferred_element_type=jnp.float32)
        if ch:
            total = total + sums[p].reshape(quarters * channels, width)
        if ch == chunks - 1:
            total = (total * scaling).T
        sums[p] = total.reshape(quarters, channels, width)
        if ch == chunks - 1:
            for n in range(quarters):
                send(p, n).start()
        return carry

    lax.fori_loop(0, count, pair_step, 0, unroll=2)


def spread_kernel(reach, chans, wins, chunks, scaling, pair_ref, p_ref, table_ref, o_ref, cross, sums,
                  t_ref, t_sem, out_sem, own_sem, s1, r1, s2, r2, s3, r3, *bufs):
    chan = lax.axis_index("chan")
    win = lax.axis_index("win")
    row = win // CORES
    core = lax.rem(win, CORES)
    rows = wins // CORES
    other = row * CORES + (CORES - 1 - core)
    own = reach - 1
    size = p_ref.shape[0] // chunks
    offsets = list(range(1 - reach, reach + 1))
    order = sorted((o for o in offsets if o != 0), key=abs)

    def at(c):
        return lax.rem(c + chans, chans)

    def peer(step):
        return lax.rem(row + step + rows, rows) * CORES + core

    friends = sorted({o % chans for o in offsets if o} | {-o % chans for o in offsets if o})
    barrier = pltpu.get_barrier_semaphore()
    for f in friends:
        pl.semaphore_signal(barrier, inc=1, device_id=(at(chan + f), win), device_id_type=MESH)
    for step in range(1, rows):
        pl.semaphore_signal(barrier, inc=1, device_id=(chan, peer(step)), device_id_type=MESH)
    pl.semaphore_signal(barrier, inc=1, device_id=(chan, other), device_id_type=MESH)
    pl.semaphore_wait(barrier, len(friends) + rows)

    def mine(ch):
        return pltpu.make_async_copy(origin(own, 0, ch), place(own, win, ch), own_sem.at[ch])

    table = pltpu.make_async_copy(table_ref, t_ref, t_sem)
    table.start()

    def place(slot, piece, ch):
        return bufs[ch].at[slot, piece]

    def origin(slot, step, ch):
        if slot == own and step == 0:
            return p_ref.at[pl.ds(ch * size, size)]
        return place(slot, peer(-step), ch)

    def whole_way(o, ch):
        return ch % 3 == min(abs(o), 2) or ch == chunks - 1

    def along(o, step, ch):
        slot = o + own
        return pltpu.make_async_remote_copy(
            src_ref=origin(own, step, ch), dst_ref=place(slot, peer(-step), ch),
            send_sem=s1.at[slot, step, ch], recv_sem=r1.at[slot, step, ch],
            device_id=(at(chan - o), win), device_id_type=MESH)

    def across(slot, step, ch):
        return pltpu.make_async_remote_copy(
            src_ref=origin(slot, 0, ch), dst_ref=place(slot, win, ch),
            send_sem=s2.at[slot, step, ch], recv_sem=r2.at[slot, step, ch],
            device_id=(chan, peer(step)), device_id_type=MESH)

    def arrived(slot, step, ch):
        here = place(slot, peer(-step), ch)
        return pltpu.make_async_remote_copy(
            src_ref=here, dst_ref=here, send_sem=s2.at[slot, step, ch],
            recv_sem=r2.at[slot, step, ch], device_id=(chan, peer(step)), device_id_type=MESH)

    def beside(slot, step, ch):
        return pltpu.make_async_remote_copy(
            src_ref=origin(slot, step, ch), dst_ref=place(slot, peer(-step), ch),
            send_sem=s3.at[slot, step, ch], recv_sem=r3.at[slot, step, ch],
            device_id=(chan, other), device_id_type=MESH)

    def from_beside(slot, step, ch):
        base = lax.rem(row - step + rows, rows) * CORES + (CORES - 1 - core)
        here = place(slot, base, ch)
        return pltpu.make_async_remote_copy(
            src_ref=here, dst_ref=here, send_sem=s3.at[slot, step, ch],
            recv_sem=r3.at[slot, step, ch], device_id=(chan, other), device_id_type=MESH)

    steps = range(1, rows)

    def begin(ch):
        for step in steps:
            across(own, step, ch).start()
        for o in order:
            along(o, 0, ch).start()
        beside(own, 0, ch).start()
        mine(ch).start()

    def send(p, n):
        return pltpu.make_async_copy(
            sums.at[p, n], o_ref.at[n % 2, 2 * p + n // 2], out_sem.at[p, n])

    def second(ch):
        for step in steps:
            arrived(own, step, ch).wait_recv()
            for o in order:
                if whole_way(o, ch):
                    along(o, step, ch).start()
            beside(own, step, ch).start()
        for o in order:
            along(o, 0, ch).wait_recv()
            if not whole_way(o, ch):
                for step in steps:
                    across(o + own, step, ch).start()
            beside(o + own, 0, ch).start()

    def third(ch):
        for o in order:
            for step in steps:
                if whole_way(o, ch):
                    along(o, step, ch).wait_recv()
                else:
                    arrived(o + own, step, ch).wait_recv()
                beside(o + own, step, ch).start()

    pick = [jnp.minimum(lax.rem(pair_ref[0, n] - (chan - own) + 2 * chans, chans), 2 * reach - 1)
            for n in range(2)]

    def compute(ch):
        if ch == 0:
            table.wait()
        mine(ch).wait()
        for o in offsets:
            for step in range(rows):
                from_beside(o + own, step, ch).wait_recv()
        cross_chunk(pick, bufs[ch], cross)
        lag_chunk(ch, chunks, scaling, t_ref, cross, sums, send)

    begin(0)
    begin(1)
    for ch in range(chunks + 2):
        if ch < chunks:
            second(ch)
        if ch + 2 < chunks:
            begin(ch + 2)
        if 0 <= ch - 1 < chunks:
            third(ch - 1)
        if ch - 2 >= 0:
            compute(ch - 2)
    for ch in range(chunks):
        for o in offsets:
            for step in range(rows):
                if o != 0 and (step == 0 or whole_way(o, ch)):
                    along(o, step, ch).wait_send()
                if step > 0 and (o == 0 or not whole_way(o, ch)):
                    across(o + own, step, ch).wait_send()
                beside(o + own, step, ch).wait_send()

    def drain(p, carry):
        for n in range(sums.shape[1]):
            send(p, n).wait()
        return carry

    lax.fori_loop(0, sums.shape[0], drain, 0)


def spread(pairs, piece, table, scaling, reach, chans, wins, chunks):
    slots = 2 * reach
    rows = wins // CORES
    groups, channels, lanes = piece.shape
    lags, bins = table.shape[0], table.shape[1] // 2
    half = channels // 2
    size = groups // chunks
    sems = pltpu.SemaphoreType.DMA((slots, rows, chunks))
    buf = pltpu.VMEM((slots, wins, size, channels, lanes), piece.dtype)
    vmem = pl.BlockSpec(memory_space=pltpu.VMEM)
    out = pl.pallas_call(
        functools.partial(spread_kernel, reach, chans, wins, chunks, scaling),
        out_shape=jax.ShapeDtypeStruct((2, half, channels, lags), jnp.float32),
        in_specs=[pl.BlockSpec(memory_space=pltpu.SMEM), vmem,
                  pl.BlockSpec(memory_space=pl.ANY)],
        out_specs=pl.BlockSpec(memory_space=pl.ANY),
        scratch_shapes=[pltpu.VMEM((half, 2, bins // chunks, 2 * channels), jnp.bfloat16),
                        pltpu.VMEM((half // 2, 4, channels, lags), jnp.float32),
                        pltpu.VMEM(table.shape, table.dtype),
                        pltpu.SemaphoreType.DMA,
                        pltpu.SemaphoreType.DMA((half // 2, 4)),
                        pltpu.SemaphoreType.DMA((chunks,))] + [sems] * 6 + [buf] * chunks,
        compiler_params=pltpu.CompilerParams(
            collective_id=0, has_side_effects=True, vmem_limit_bytes=56 * 2**20),
        name="spread",
    )(pairs, piece, table)
    return out.reshape(1, channels, channels, lags)


def per_device(chans, wins, spectra, pair_blocks):
    whitened = whiten(spectra)
    length_bins = spectra.shape[3]
    reach = pair_blocks.shape[0] * wins // 2
    chunks = 8 if wins <= 2 * CORES else 4
    table = make_table(length_bins).reshape(NLAG, 2, chunks, -1).transpose(0, 2, 1, 3)
    table = jnp.asarray(table.reshape(NLAG, 2 * length_bins))
    scaling = 1.0 / math.sqrt(spectra.shape[1] * wins * length_bins)
    return spread(pair_blocks, arrange(whitened), table, scaling, reach, chans, wins, chunks)


def solution(mesh):
    in_specs = (P(None, "win", "chan", None), P(("chan", "win"), None))
    out_specs = P(("chan", "win"), None, None, None)
    return jax.shard_map(
        functools.partial(per_device, mesh.shape["chan"], mesh.shape["win"]),
        mesh=mesh, in_specs=in_specs, out_specs=out_specs, check_vma=False
    )
```
